32 devices in a mesh: groups: 2 (over y), units: 8 (over z, x), heads: 2 (over core).
Axes of the slice: x: 2, y: 2, z: 4, core: 2. Of those that a mesh axis runs over, the one named last changes fastest.
Arguments:
- queries: bfloat16 [16, 6144], P(('groups', 'units'), 'heads'), parts along dimension 0, may hold values from -160 to 160
- fresh_key: bfloat16 [16, 1024], P(('groups', 'units'), 'heads'), parts along dimension 0, may hold values from -6 to 6
- fresh_value: bfloat16 [16, 1024], P(('groups', 'units'), 'heads'), parts along dimension 0, may hold values from -6 to 6
- key_cache_pages: bfloat16 [64, 128, 1024], P(('groups', 'units'), None, 'heads'), parts along dimension 0, may hold values from -6 to 6
- value_cache_pages: bfloat16 [64, 128, 1024], P(('groups', 'units'), None, 'heads'), parts along dimension 0, may hold values from -6 to 6
- page_table: int32 [16, 4], P(('groups', 'units')), parts along dimension 0, may hold values from 0 to 3, as said below
- lengths: int32 [16], P(('groups', 'units')), parts along dimension 0, may hold values from 1 to 512, as said below
- resid: bfloat16 [16, 6144], P('groups', 'units'), parts along dimension 0, may hold values from -0.59765625 to 0.59765625
- w_out: bfloat16 [6144, 6144], P('heads', 'units'), may hold values from -0.078125 to 0.078125
- norm_gain: bfloat16 [6144], replicated, may hold values from 0.25 to 1.75
- router: bfloat16 [6144, 8], replicated, may hold values from -0.15625 to 0.15625
- routes: int32 [16, 2], P('groups'), parts along dimension 0, may hold values from 0 to 7, as said below
- w_gate: bfloat16 [6144, 16384], P('heads', 'units'), may hold values from -0.078125 to 0.078125
- w_up: bfloat16 [6144, 16384], P('heads', 'units'), may hold values from -0.078125 to 0.078125
- w_down: bfloat16 [16384, 6144], P('units', 'heads'), may hold values from -0.09375 to 0.09375
Outputs:
- layer_out: bfloat16 [16, 6144], P(('groups', 'units'), 'heads'), parts along dimension 0
The draws below stay inside these ranges and needn't reach their ends.
There are 2 independent parts, one for each index of `groups`. The reference program is written for one: setup_inputs(seed, part) draws one part's arguments, and reference() takes and returns one part's arrays. A program takes and returns all parts, laid end to end along the dimension named above; an argument that names none is the same for every part. Nothing has to cross between parts.
Inputs may be any that keep to these rules, and one draw needn't show every extreme that they name: `page_table`: the 1 requests r of one pool block b = r // 1 use every page of that block exactly once among them. `lengths`: some request has exactly 512 cached tokens. `routes`: each request names two different experts; exactly 2 requests name expert 0.
All inputs are finite; a program needn't handle non-finite values.
Results may differ from the reference program's by a relative error of at most 0.01.
Values may be sent and summed in bfloat16 or wider, within the bound.
No kernel may reach another device: no remote copies, remote signals or barrier semaphores. Data moves between devices by JAX's collectives and lax.ppermute only.
A program may use at most 128 MiB of HBM per device.

```python
import jax
import jax.numpy as jnp
from jax import lax

D = 6144
QUERY_HEADS = 48
KEY_VALUE_HEADS = 8
HEAD_WIDTH = 128
FF = 16384
EXPERTS = 8
PAGE_TOKENS = 128
PAGES = 4
REQ_DEV = 1
CTX = 512
REQUEST_COUNT = 8
ROUTED = 2
CACHE_PAGES = 32
N_UNITS = 8


def draw_queries(key, part):
    key = jax.random.fold_in(key, 11)
    base_key = jax.random.fold_in(key, 0)
    base = jnp.clip(jax.random.normal(base_key, (REQUEST_COUNT, QUERY_HEADS, HEAD_WIDTH), jnp.float32), -4.0, 4.0)
    return base.reshape(REQUEST_COUNT, QUERY_HEADS * HEAD_WIDTH).astype(jnp.bfloat16)


def draw_page_table(key, part):
    key = jax.random.fold_in(key, 23)
    key_rows = jax.random.split(key, N_UNITS)
    block = PAGES * REQ_DEV
    perms = jax.vmap(lambda k: jax.random.permutation(k, jnp.arange(block, dtype=jnp.int32)))(key_rows)
    return perms.reshape(REQUEST_COUNT, PAGES).astype(jnp.int32)


def draw_lengths(key, part):
    key = jax.random.fold_in(key, 37)
    len_key, pick_key = jax.random.split(key)
    drawn = jax.random.randint(len_key, (REQUEST_COUNT,), 1, CTX + 1, jnp.int32)
    chosen = jax.random.randint(pick_key, (), 0, REQUEST_COUNT, jnp.int32)
    return drawn.at[chosen].set(CTX)


def draw_routes(key, part):
    key = jax.random.fold_in(key, 41)
    perm_key, first_key, step_key, swap_key = jax.random.split(key, 4)
    order = jax.random.permutation(perm_key, jnp.arange(REQUEST_COUNT, dtype=jnp.int32))
    picked = order < ROUTED
    first = jax.random.randint(first_key, (REQUEST_COUNT,), 1, EXPERTS, jnp.int32)
    step = jax.random.randint(step_key, (REQUEST_COUNT,), 1, EXPERTS - 1, jnp.int32)
    second = 1 + (first - 1 + step) % (EXPERTS - 1)
    swap = jax.random.randint(swap_key, (REQUEST_COUNT,), 0, 2, jnp.int32)
    zero = jnp.zeros((REQUEST_COUNT,), jnp.int32)
    col_a = jnp.where(picked, jnp.where(swap == 0, zero, first), first)
    col_b = jnp.where(picked, jnp.where(swap == 0, first, zero), second)
    return jnp.stack([col_a, col_b], axis=1).astype(jnp.int32)


def shard_levels(key, dims, pieces, smallest, high):
    factor_of, own = 1.0, jax.random.fold_in(key, 6)
    for position, parts in pieces:
        heights = jnp.exp(jax.random.uniform(jax.random.fold_in(own, position), (parts,), jnp.float32, smallest / len(pieces), high / len(pieces)))
        factor_of = factor_of * jnp.repeat(heights, dims[position] // parts).reshape([-1 if axis == position else 1 for axis in range(len(dims))])
    return factor_of


def scatter_about(own_key, shape, spread, most, shards=(), kind=jnp.bfloat16):
    array = spread * jax.random.normal(own_key, shape, jnp.float32)
    if shards:
        array = array * shard_levels(own_key, shape, shards, -0.22, 0.18)
    return jnp.clip(array, -most, most).astype(kind)


def setup_inputs(seed: int = 0, part: int = 0) -> dict:
    key_of = jax.random.split(jax.random.key(seed), 16)
    part_splits = jax.random.split(jax.random.fold_in(key_of[15], part), 16)
    return {
        "queries": draw_queries(jax.random.fold_in(jax.random.fold_in(key_of[15], part), 71), part),
        "fresh_key": scatter_about(part_splits[1], (REQUEST_COUNT, KEY_VALUE_HEADS * HEAD_WIDTH), 1.0, 6.0, ((0, 8), (1, 2))),
        "fresh_value": scatter_about(part_splits[2], (REQUEST_COUNT, KEY_VALUE_HEADS * HEAD_WIDTH), 1.0, 6.0, ((0, 8), (1, 2))),
        "key_cache_pages": scatter_about(part_splits[3], (CACHE_PAGES, PAGE_TOKENS, KEY_VALUE_HEADS * HEAD_WIDTH), 1.0, 6.0, ((0, 8), (2, 2))),
        "value_cache_pages": scatter_about(part_splits[4], (CACHE_PAGES, PAGE_TOKENS, KEY_VALUE_HEADS * HEAD_WIDTH), 1.0, 6.0, ((0, 8), (2, 2))),
        "page_table": draw_page_table(jax.random.fold_in(jax.random.fold_in(key_of[15], part), 71), part),
        "lengths": draw_lengths(jax.random.fold_in(jax.random.fold_in(key_of[15], part), 71), part),
        "resid": scatter_about(part_splits[7], (REQUEST_COUNT, D), 0.1, 0.59765625, ((1, 8),)),
        "w_out": scatter_about(key_of[8], (QUERY_HEADS * HEAD_WIDTH, D), (QUERY_HEADS * HEAD_WIDTH) ** -0.5, 0.078125, ((0, 2), (1, 8))),
        "norm_gain": jnp.clip(1.0 + 0.15 * jax.random.normal(key_of[9], (D,), jnp.float32), 0.25, 1.75).astype(jnp.bfloat16),
        "router": scatter_about(key_of[10], (D, EXPERTS), (D // 4) ** -0.5, 0.15625),
        "routes": draw_routes(jax.random.fold_in(jax.random.fold_in(key_of[15], part), 71), part),
        "w_gate": scatter_about(key_of[12], (D, FF), D ** -0.5, 0.078125, ((0, 2), (1, 8))),
        "w_up": scatter_about(key_of[13], (D, FF), D ** -0.5, 0.078125, ((0, 2), (1, 8))),
        "w_down": scatter_about(key_of[14], (FF, D), (FF // 4) ** -0.5, 0.09375, ((0, 8), (1, 2))),
    }


def attend(queries, fresh_key, fresh_value, key_rows, value_rows, lengths):
    token_rows = queries.shape[0]
    query_group = QUERY_HEADS // KEY_VALUE_HEADS
    score_scale = HEAD_WIDTH ** (-0.5)
    query_rows = queries.reshape(token_rows, KEY_VALUE_HEADS, query_group, HEAD_WIDTH).astype(jnp.float32)
    key_rows = key_rows.reshape(token_rows, -1, KEY_VALUE_HEADS, HEAD_WIDTH).astype(jnp.float32)
    value_rows = value_rows.reshape(token_rows, -1, KEY_VALUE_HEADS, HEAD_WIDTH).astype(jnp.float32)
    scores = jnp.einsum('rgjd,rtgd->rgjt', query_rows, key_rows) * score_scale
    expert_owned = jnp.einsum('fiam,fim->fia', query_rows, fresh_key.reshape(token_rows, KEY_VALUE_HEADS, HEAD_WIDTH).astype(jnp.float32)) * score_scale
    span = key_rows.shape[1]
    live = (jnp.arange(span, dtype=jnp.int32)[None, :] < lengths[:, None])[:, None, None, :]
    top = jnp.maximum(lax.optimization_barrier(jnp.max(jnp.where(live, scores, -jnp.inf), axis=-1)), expert_owned)
    prob = jnp.where(live, jnp.exp(scores - top[..., None]), 0.0)
    own_p = jnp.exp(expert_owned - top)
    total = lax.optimization_barrier(jnp.sum(prob, axis=-1)) + own_p
    weights = (prob / total[..., None]).astype(jnp.bfloat16)
    owned_weight = (own_p / total).astype(jnp.bfloat16)
    blended_values = jnp.einsum('rgjt,rtgd->rgjd', weights.astype(jnp.float32), value_rows)
    blended_values = blended_values + owned_weight.astype(jnp.float32)[..., None] * fresh_value.reshape(token_rows, KEY_VALUE_HEADS, 1, HEAD_WIDTH).astype(jnp.float32)
    return blended_values.reshape(token_rows, QUERY_HEADS * HEAD_WIDTH).astype(jnp.bfloat16)

def route_weight(logits, routes):
    picks = (routes[:, :, None] == jnp.arange(logits.shape[1], dtype=jnp.int32)[None, None, :]).astype(jnp.float32)
    chosen = lax.optimization_barrier(jnp.sum(picks * logits[:, None, :], axis=-1))
    first = jax.nn.sigmoid(chosen[:, 0] - chosen[:, 1])
    second = jax.nn.sigmoid(chosen[:, 1] - chosen[:, 0])
    return jnp.where(routes[:, 0] == 0, first, jnp.where(routes[:, 1] == 0, second, 0.0))

def reference(queries, fresh_key, fresh_value, key_cache_pages, value_cache_pages, page_table, lengths, resid, w_out, norm_gain, router, routes, w_gate, w_up, w_down):
    block = jnp.arange(REQUEST_COUNT, dtype=jnp.int32) // REQ_DEV * (PAGES * REQ_DEV)
    pages = (block[:, None] + page_table).astype(jnp.int32)
    key_rows = key_cache_pages[pages]
    value_rows = value_cache_pages[pages]
    attn = attend(queries, fresh_key, fresh_value, key_rows, value_rows, lengths)
    proj = jnp.dot(attn, w_out, preferred_element_type=jnp.float32)
    h1 = (resid.astype(jnp.float32) + proj).astype(jnp.bfloat16)
    hf = h1.astype(jnp.float32)
    rstd = lax.rsqrt(lax.optimization_barrier(jnp.mean(hf * hf, axis=-1, keepdims=True)) + 1e-05)
    xn = (hf * rstd * norm_gain.astype(jnp.float32)).astype(jnp.bfloat16)
    logits = jnp.dot(xn, router, preferred_element_type=jnp.float32)
    route = route_weight(logits, routes)
    gate = jnp.dot(xn, w_gate, preferred_element_type=jnp.float32)
    up = jnp.dot(xn, w_up, preferred_element_type=jnp.float32)
    hidden = (jax.nn.silu(gate) * up * route[:, None]).astype(jnp.bfloat16)
    moe = jnp.dot(hidden, w_down, preferred_element_type=jnp.float32)
    return (hf + moe).astype(jnp.bfloat16)
```

```python
import functools

import jax
import jax.numpy as jnp
from jax import lax
from jax.experimental import pallas as pl
from jax.experimental.pallas import tpu as pltpu
from jax.sharding import PartitionSpec as P

HEAD_WIDTH = 128
LANES = 128
F32 = jnp.float32
BF16 = jnp.bfloat16
MIB = 2**20


def attend(
    queries, fresh_key, fresh_value, key_cache_pages, value_cache_pages, page_table, lengths
):
    token_rows = queries.shape[0]
    kv_width = fresh_key.shape[1]
    heads_kv = kv_width // HEAD_WIDTH
    query_group = queries.shape[1] // kv_width
    score_scale = HEAD_WIDTH ** (-0.5)
    key_rows = key_cache_pages[page_table].reshape(token_rows, -1, heads_kv, HEAD_WIDTH)
    value_rows = value_cache_pages[page_table].reshape(token_rows, -1, heads_kv, HEAD_WIDTH)
    query_grid = queries.reshape(token_rows, heads_kv, query_group, HEAD_WIDTH)
    scores = (
        jnp.einsum("rgjd,rtgd->rgjt", query_grid, key_rows, preferred_element_type=jnp.float32)
        * score_scale
    )
    expert_owned = (
        jnp.einsum(
            "fiam,fim->fia",
            query_grid,
            fresh_key.reshape(token_rows, heads_kv, HEAD_WIDTH),
            preferred_element_type=jnp.float32,
        )
        * score_scale
    )
    span = key_rows.shape[1]
    live = (jnp.arange(span, dtype=jnp.int32)[None, :] < lengths[:, None])[:, None, None, :]
    top = jnp.maximum(jnp.max(jnp.where(live, scores, -jnp.inf), axis=-1), expert_owned)
    prob = jnp.where(live, jnp.exp(scores - top[..., None]), 0.0)
    own_p = jnp.exp(expert_owned - top)
    total = jnp.sum(prob, axis=-1) + own_p
    weights = (prob / total[..., None]).astype(jnp.bfloat16)
    owned_weight = (own_p / total).astype(jnp.bfloat16)
    blended_values = jnp.einsum(
        "rgjt,rtgd->rgjd", weights, value_rows, preferred_element_type=jnp.float32
    )
    blended_values = blended_values + owned_weight.astype(jnp.float32)[
        ..., None
    ] * fresh_value.reshape(token_rows, heads_kv, 1, HEAD_WIDTH).astype(jnp.float32)
    return blended_values.reshape(token_rows, -1).astype(jnp.bfloat16)


def route_weight(logits, routes):
    picks = (
        routes[:, :, None] == jnp.arange(logits.shape[1], dtype=jnp.int32)[None, None, :]
    ).astype(jnp.float32)
    chosen = jnp.sum(picks * logits[:, None, :], axis=-1)
    first = jax.nn.sigmoid(chosen[:, 0] - chosen[:, 1])
    second = jax.nn.sigmoid(chosen[:, 1] - chosen[:, 0])
    return jnp.where(routes[:, 0] == 0, first, jnp.where(routes[:, 1] == 0, second, 0.0))


def body(
    queries,
    fresh_key,
    fresh_value,
    key_cache_pages,
    value_cache_pages,
    page_table,
    lengths,
    resid,
    w_out,
    norm_gain,
    router,
    routes,
    w_gate,
    w_up,
    w_down,
):
    own_rows = queries.shape[0]
    half_width = w_gate.shape[0]
    all_rows = routes.shape[0]
    routed_count = all_rows * routes.shape[1] // router.shape[1]
    unit_index = lax.axis_index("units")
    head_index = lax.axis_index("heads")
    attn = attend(
        queries, fresh_key, fresh_value, key_cache_pages, value_cache_pages, page_table, lengths
    )
    proj_part = jnp.dot(
        lax.all_gather(attn, "units", axis=0, tiled=True), w_out, preferred_element_type=jnp.float32
    )
    proj = lax.psum(proj_part, "heads")
    h1_cols = (resid.astype(jnp.float32) + proj).astype(jnp.bfloat16)
    h1 = lax.all_gather(h1_cols, "units", axis=1, tiled=True)
    is_routed = jnp.any(routes == 0, axis=1)
    slot_of = jnp.cumsum(is_routed.astype(jnp.int32)) - 1
    slot_ids = jnp.arange(routed_count, dtype=jnp.int32)
    row_ids = jnp.arange(all_rows, dtype=jnp.int32)
    match = (slot_of[None, :] == slot_ids[:, None]) & is_routed[None, :]
    picked_rows = jnp.sum(jnp.where(match, row_ids[None, :], 0), axis=1)
    h1_sel = h1[picked_rows]
    hf_sel = h1_sel.astype(jnp.float32)
    rstd = lax.rsqrt(jnp.mean(hf_sel * hf_sel, axis=-1, keepdims=True) + 1e-05)
    xn_sel = (hf_sel * rstd * norm_gain.astype(jnp.float32)).astype(jnp.bfloat16)
    logits = jnp.dot(xn_sel, router, preferred_element_type=jnp.float32)
    route = route_weight(logits, routes[picked_rows])
    xn_half = lax.dynamic_slice_in_dim(xn_sel, head_index * half_width, half_width, 1)
    gate_part = jnp.dot(xn_half, w_gate, preferred_element_type=jnp.float32)
    up_part = jnp.dot(xn_half, w_up, preferred_element_type=jnp.float32)
    gate, up = lax.psum((gate_part, up_part), "heads")
    hidden = (jax.nn.silu(gate) * up * route[:, None]).astype(jnp.bfloat16)
    full_term = jnp.dot(hidden, w_down, preferred_element_type=jnp.float32)
    own_start = unit_index * own_rows
    own_h1 = lax.dynamic_slice_in_dim(
        lax.dynamic_slice_in_dim(h1, own_start, own_rows, 0), head_index * half_width, half_width, 1
    )
    own_routed = lax.dynamic_slice_in_dim(is_routed, own_start, own_rows, 0)
    own_slot = jnp.maximum(lax.dynamic_slice_in_dim(slot_of, own_start, own_rows, 0), 0)
    moe_sel = lax.psum(full_term, "units")
    moe_own = jnp.where(own_routed[:, None], moe_sel[own_slot], 0.0)
    return (own_h1.astype(jnp.float32) + moe_own).astype(jnp.bfloat16)


def attn_kernel(table_ref, len_ref, q_ref, fk_ref, fv_ref, k_ref, v_ref, o_ref):
    pages, page_tokens, kv_width = k_ref.shape
    heads_kv = kv_width // HEAD_WIDTH
    group = q_ref.shape[1] // kv_width
    rows = -(-group // 8) * 8
    span = pages * page_tokens
    scale = HEAD_WIDTH ** (-0.5)
    length = len_ref[0]
    q = q_ref[...].astype(F32)
    fk = fk_ref[...].astype(F32)
    fv = fv_ref[...].astype(F32)
    pad = [jnp.zeros((rows - group, HEAD_WIDTH), F32)] if rows > group else []
    live = lax.broadcasted_iota(jnp.int32, (rows, span), 1) < length
    blended = []
    for g in range(heads_kv):
        lanes = slice(g * HEAD_WIDTH, (g + 1) * HEAD_WIDTH)
        first = g * group
        q_g = jnp.concatenate(
            [q[:, (first + j) * HEAD_WIDTH : (first + j + 1) * HEAD_WIDTH] for j in range(group)] + pad,
            axis=0,
        )
        keys = jnp.concatenate([k_ref[table_ref[0, p], :, lanes] for p in range(pages)], axis=0)
        values = jnp.concatenate([v_ref[table_ref[0, p], :, lanes] for p in range(pages)], axis=0)
        s = (
            lax.dot_general(
                q_g.astype(BF16), keys, (((1,), (1,)), ((), ())), preferred_element_type=F32
            )
            * scale
        )
        own = jnp.sum(q_g * fk[:, lanes], axis=1, keepdims=True) * scale
        top = jnp.maximum(jnp.max(jnp.where(live, s, -jnp.inf), axis=1, keepdims=True), own)
        prob = jnp.where(live, jnp.exp(s - top), 0.0)
        own_p = jnp.exp(own - top)
        total = jnp.sum(prob, axis=1, keepdims=True) + own_p
        weights = (prob / total).astype(BF16)
        own_weight = (own_p / total).astype(BF16).astype(F32)
        out = jnp.dot(weights, values, preferred_element_type=F32) + own_weight * fv[:, lanes]
        blended.append(out[:group])
    attn = jnp.concatenate(blended, axis=0).astype(BF16)
    for r in range(o_ref.shape[0]):
        o_ref[r] = attn


def proj_kernel(attn_ref, w_ref, o_ref):
    attn = attn_ref[...].astype(F32)
    x = jnp.concatenate([attn[:, j, :] for j in range(attn.shape[1])], axis=1).astype(BF16)
    o_ref[...] = jnp.dot(x, w_ref[...], preferred_element_type=F32)


def resid_kernel(resid_ref, mine_ref, other_ref, o_ref):
    h1 = (resid_ref[...].astype(F32) + (mine_ref[...] + other_ref[...])).astype(BF16)
    for r in range(o_ref.shape[0]):
        o_ref[r] = h1


def routed_rows(routes_ref):
    count = routes_ref.shape[0]
    first = jnp.int32(count - 1)
    last = jnp.int32(0)
    for r in range(count):
        hit = jnp.logical_or(routes_ref[r, 0] == 0, routes_ref[r, 1] == 0)
        first = jnp.where(hit, jnp.minimum(first, r), first)
        last = jnp.where(hit, r, last)
    return first, last


def expert_kernel(
    routes_ref, h1_ref, gain_ref, router_ref, routes_v_ref, wg_ref, wu_ref, gu_ref, route_ref, own_ref,
    gu_all, route_all, own_all,
):
    units = h1_ref.shape[0]
    half = wg_ref.shape[0]
    hidden = wg_ref.shape[1]
    head = lax.axis_index("heads")
    unit = lax.axis_index("units")
    h1 = jnp.concatenate([h1_ref[u] for u in range(units)], axis=1).astype(F32)
    gain = gain_ref[...].astype(F32)
    rstd = lax.rsqrt(jnp.mean(h1 * h1, axis=1, keepdims=True) + 1e-05)
    xn = (h1 * rstd * gain).astype(BF16)
    x_half = jnp.where(head == 0, xn[:, :half].astype(F32), xn[:, half:].astype(F32)).astype(BF16)
    own_all[...] = jnp.where(head == 0, h1[:, :half], h1[:, half:])
    own_ref[...] = own_all[pl.ds(unit, 1), :]
    gu_all[:, :hidden] = jnp.dot(x_half, wg_ref[...], preferred_element_type=F32)
    gu_all[:, hidden:] = jnp.dot(x_half, wu_ref[...], preferred_element_type=F32)
    logits = jnp.dot(xn, router_ref[...], preferred_element_type=F32)
    expert_ids = lax.broadcasted_iota(jnp.int32, logits.shape, 1)
    one = routes_v_ref[:, 0:1]
    two = routes_v_ref[:, 1:2]
    chosen_one = jnp.sum(jnp.where(expert_ids == one, logits, 0.0), axis=1, keepdims=True)
    chosen_two = jnp.sum(jnp.where(expert_ids == two, logits, 0.0), axis=1, keepdims=True)
    diff = jnp.where(one == 0, chosen_one - chosen_two, chosen_two - chosen_one)
    route = jnp.where(jnp.logical_or(one == 0, two == 0), 1.0 / (1.0 + jnp.exp(-diff)), 0.0)
    route_all[...] = jnp.broadcast_to(route, route_all.shape)
    for slot, r in enumerate(routed_rows(routes_ref)):
        gu_ref[slot : slot + 1, :] = gu_all[pl.ds(r, 1), :]
        route_ref[slot : slot + 1, :] = route_all[pl.ds(r, 1), :]


def down_kernel(routes_ref, mine_ref, other_ref, route_ref, wd_ref, o_ref):
    hidden = wd_ref.shape[0]
    gu = mine_ref[...] + other_ref[...]
    gate = gu[:, :hidden]
    up = gu[:, hidden:]
    act = (gate / (1.0 + jnp.exp(-gate)) * up * route_ref[:, 0:1]).astype(BF16)
    full = jnp.dot(act, wd_ref[...], preferred_element_type=F32)
    o_ref[...] = jnp.zeros(o_ref.shape, F32)
    for slot, r in enumerate(routed_rows(routes_ref)):
        for j in range(o_ref.shape[1]):
            o_ref[r, j : j + 1, :] = full[slot : slot + 1, j * LANES : (j + 1) * LANES]


def sum_kernel(parts_ref, own_ref, o_ref):
    moe = parts_ref[0]
    for u in range(1, parts_ref.shape[0]):
        moe = moe + parts_ref[u]
    for j in range(parts_ref.shape[1]):
        lanes = slice(j * LANES, (j + 1) * LANES)
        o_ref[:, lanes] = (own_ref[:, lanes] + moe[j : j + 1, :]).astype(o_ref.dtype)


SMEM = pl.BlockSpec(memory_space=pltpu.SMEM)
VMEM = pl.BlockSpec(memory_space=pltpu.VMEM)


def in_vmem(x):
    return pltpu.with_memory_space_constraint(x, pltpu.VMEM)


def small_body(
    queries,
    fresh_key,
    fresh_value,
    key_cache_pages,
    value_cache_pages,
    page_table,
    lengths,
    resid,
    w_out,
    norm_gain,
    router,
    routes,
    w_gate,
    w_up,
    w_down,
):
    rows = routes.shape[0]
    half = w_gate.shape[0]
    chunks = half // LANES
    hidden = w_gate.shape[1]
    cols = w_out.shape[1]
    swap = [(0, 1), (1, 0)]

    def exchange(x):
        return lax.all_to_all(x, "units", split_axis=0, concat_axis=0, tiled=True)

    def call(kernel, out, specs, name, scratch=(), limit=6):
        return pl.pallas_call(
            kernel,
            out_shape=out,
            in_specs=specs,
            out_specs=jax.tree.map(lambda _: VMEM, out),
            scratch_shapes=scratch,
            compiler_params=pltpu.CompilerParams(vmem_limit_bytes=limit * MIB),
            name=name,
        )

    attn = call(
        attn_kernel,
        jax.ShapeDtypeStruct((rows, chunks, LANES), BF16),
        [SMEM, SMEM, VMEM, VMEM, VMEM, VMEM, VMEM],
        "attend",
    )(
        page_table, lengths, queries, fresh_key, fresh_value,
        in_vmem(key_cache_pages), in_vmem(value_cache_pages),
    )
    attn_all = exchange(attn)
    proj = call(proj_kernel, jax.ShapeDtypeStruct((rows, cols), F32), [VMEM] * 2, "proj")(
        attn_all, in_vmem(w_out)
    )
    proj_other = lax.ppermute(proj, "heads", swap)
    h1_cols = call(
        resid_kernel, jax.ShapeDtypeStruct((rows, rows, cols), BF16), [VMEM] * 3, "resid"
    )(resid, proj, proj_other)
    h1 = exchange(h1_cols)
    gu, route, own_h1 = call(
        expert_kernel,
        (
            jax.ShapeDtypeStruct((2, 2 * hidden), F32),
            jax.ShapeDtypeStruct((2, LANES), F32),
            jax.ShapeDtypeStruct((1, half), F32),
        ),
        [SMEM] + [VMEM] * 6,
        "expert",
        scratch=(
            pltpu.VMEM((rows, 2 * hidden), F32),
            pltpu.VMEM((rows, LANES), F32),
            pltpu.VMEM((rows, half), F32),
        ),
    )(
        routes, h1, norm_gain.reshape(1, -1), in_vmem(router), routes, in_vmem(w_gate), in_vmem(w_up)
    )
    gu_other = lax.ppermute(gu, "heads", swap)
    full = call(
        down_kernel,
        jax.ShapeDtypeStruct((rows, chunks, LANES), F32),
        [SMEM] + [VMEM] * 4,
        "down",
    )(routes, gu, gu_other, route, in_vmem(w_down))
    parts = exchange(full)
    return call(sum_kernel, jax.ShapeDtypeStruct((1, half), BF16), [VMEM] * 2, "total")(
        parts, own_h1
    )


def one_tile(*args):
    queries, routes, router = args[0], args[11], args[10]
    rows = routes.shape[0]
    units = lax.axis_size("units")
    return (
        queries.shape[0] == 1
        and rows == 8
        and units == rows
        and rows * routes.shape[1] // router.shape[1] == 2
    )


def dispatch(*args):
    return small_body(*args) if one_tile(*args) else body(*args)


def solution(mesh):
    in_specs = (
        P(("groups", "units"), "heads"),
        P(("groups", "units"), "heads"),
        P(("groups", "units"), "heads"),
        P(("groups", "units"), None, "heads"),
        P(("groups", "units"), None, "heads"),
        P(("groups", "units"), None),
        P(("groups", "units")),
        P("groups", "units"),
        P("heads", "units"),
        P(),
        P(),
        P("groups", None),
        P("heads", "units"),
        P("heads", "units"),
        P("units", "heads"),
    )
    out_specs = P(("groups", "units"), "heads")
    return jax.shard_map(dispatch, mesh=mesh, in_specs=in_specs, out_specs=out_specs, check_vma=False)
```

```python
import functools

import jax
import jax.numpy as jnp
from jax import lax
from jax.experimental import pallas as pl
from jax.experimental.pallas import tpu as pltpu
from jax.sharding import PartitionSpec as P

HEAD_WIDTH = 128
LANES = 128
F32 = jnp.float32
BF16 = jnp.bfloat16
MIB = 2**20


def attend(
    queries, fresh_key, fresh_value, key_cache_pages, value_cache_pages, page_table, lengths
):
    token_rows = queries.shape[0]
    kv_width = fresh_key.shape[1]
    heads_kv = kv_width // HEAD_WIDTH
    query_group = queries.shape[1] // kv_width
    score_scale = HEAD_WIDTH ** (-0.5)
    key_rows = key_cache_pages[page_table].reshape(token_rows, -1, heads_kv, HEAD_WIDTH)
    value_rows = value_cache_pages[page_table].reshape(token_rows, -1, heads_kv, HEAD_WIDTH)
    query_grid = queries.reshape(token_rows, heads_kv, query_group, HEAD_WIDTH)
    scores = (
        jnp.einsum("rgjd,rtgd->rgjt", query_grid, key_rows, preferred_element_type=jnp.float32)
        * score_scale
    )
    expert_owned = (
        jnp.einsum(
            "fiam,fim->fia",
            query_grid,
            fresh_key.reshape(token_rows, heads_kv, HEAD_WIDTH),
            preferred_element_type=jnp.float32,
        )
        * score_scale
    )
    span = key_rows.shape[1]
    live = (jnp.arange(span, dtype=jnp.int32)[None, :] < lengths[:, None])[:, None, None, :]
    top = jnp.maximum(jnp.max(jnp.where(live, scores, -jnp.inf), axis=-1), expert_owned)
    prob = jnp.where(live, jnp.exp(scores - top[..., None]), 0.0)
    own_p = jnp.exp(expert_owned - top)
    total = jnp.sum(prob, axis=-1) + own_p
    weights = (prob / total[..., None]).astype(jnp.bfloat16)
    owned_weight = (own_p / total).astype(jnp.bfloat16)
    blended_values = jnp.einsum(
        "rgjt,rtgd->rgjd", weights, value_rows, preferred_element_type=jnp.float32
    )
    blended_values = blended_values + owned_weight.astype(jnp.float32)[
        ..., None
    ] * fresh_value.reshape(token_rows, heads_kv, 1, HEAD_WIDTH).astype(jnp.float32)
    return blended_values.reshape(token_rows, -1).astype(jnp.bfloat16)


def route_weight(logits, routes):
    picks = (
        routes[:, :, None] == jnp.arange(logits.shape[1], dtype=jnp.int32)[None, None, :]
    ).astype(jnp.float32)
    chosen = jnp.sum(picks * logits[:, None, :], axis=-1)
    first = jax.nn.sigmoid(chosen[:, 0] - chosen[:, 1])
    second = jax.nn.sigmoid(chosen[:, 1] - chosen[:, 0])
    return jnp.where(routes[:, 0] == 0, first, jnp.where(routes[:, 1] == 0, second, 0.0))


def body(
    queries,
    fresh_key,
    fresh_value,
    key_cache_pages,
    value_cache_pages,
    page_table,
    lengths,
    resid,
    w_out,
    norm_gain,
    router,
    routes,
    w_gate,
    w_up,
    w_down,
):
    own_rows = queries.shape[0]
    half_width = w_gate.shape[0]
    all_rows = routes.shape[0]
    routed_count = all_rows * routes.shape[1] // router.shape[1]
    unit_index = lax.axis_index("units")
    head_index = lax.axis_index("heads")
    attn = attend(
        queries, fresh_key, fresh_value, key_cache_pages, value_cache_pages, page_table, lengths
    )
    proj_part = jnp.dot(
        lax.all_gather(attn, "units", axis=0, tiled=True), w_out, preferred_element_type=jnp.float32
    )
    proj = lax.psum(proj_part, "heads")
    h1_cols = (resid.astype(jnp.float32) + proj).astype(jnp.bfloat16)
    h1 = lax.all_gather(h1_cols, "units", axis=1, tiled=True)
    is_routed = jnp.any(routes == 0, axis=1)
    slot_of = jnp.cumsum(is_routed.astype(jnp.int32)) - 1
    slot_ids = jnp.arange(routed_count, dtype=jnp.int32)
    row_ids = jnp.arange(all_rows, dtype=jnp.int32)
    match = (slot_of[None, :] == slot_ids[:, None]) & is_routed[None, :]
    picked_rows = jnp.sum(jnp.where(match, row_ids[None, :], 0), axis=1)
    h1_sel = h1[picked_rows]
    hf_sel = h1_sel.astype(jnp.float32)
    rstd = lax.rsqrt(jnp.mean(hf_sel * hf_sel, axis=-1, keepdims=True) + 1e-05)
    xn_sel = (hf_sel * rstd * norm_gain.astype(jnp.float32)).astype(jnp.bfloat16)
    logits = jnp.dot(xn_sel, router, preferred_element_type=jnp.float32)
    route = route_weight(logits, routes[picked_rows])
    xn_half = lax.dynamic_slice_in_dim(xn_sel, head_index * half_width, half_width, 1)
    gate_part = jnp.dot(xn_half, w_gate, preferred_element_type=jnp.float32)
    up_part = jnp.dot(xn_half, w_up, preferred_element_type=jnp.float32)
    gate, up = lax.psum((gate_part, up_part), "heads")
    hidden = (jax.nn.silu(gate) * up * route[:, None]).astype(jnp.bfloat16)
    full_term = jnp.dot(hidden, w_down, preferred_element_type=jnp.float32)
    own_start = unit_index * own_rows
    own_h1 = lax.dynamic_slice_in_dim(
        lax.dynamic_slice_in_dim(h1, own_start, own_rows, 0), head_index * half_width, half_width, 1
    )
    own_routed = lax.dynamic_slice_in_dim(is_routed, own_start, own_rows, 0)
    own_slot = jnp.maximum(lax.dynamic_slice_in_dim(slot_of, own_start, own_rows, 0), 0)
    moe_sel = lax.psum(full_term, "units")
    moe_own = jnp.where(own_routed[:, None], moe_sel[own_slot], 0.0)
    return (own_h1.astype(jnp.float32) + moe_own).astype(jnp.bfloat16)


def attn_kernel(
    len_ref, table_hbm, q_hbm, fk_hbm, fv_hbm, k_hbm, v_hbm, o_ref,
    table_ref, q_ref, fk_ref, fv_ref, k_ref, v_ref, sems,
):
    copies = [
        pltpu.make_async_copy(src, dst, sems.at[i])
        for i, (src, dst) in enumerate(
            (
                (table_hbm, table_ref),
                (q_hbm, q_ref),
                (fk_hbm, fk_ref),
                (k_hbm, k_ref),
                (v_hbm, v_ref),
                (fv_hbm, fv_ref),
            )
        )
    ]
    for copy in copies:
        copy.start()
    for copy in copies:
        copy.wait()
    pages, page_tokens, kv_width = k_ref.shape
    heads_kv = kv_width // HEAD_WIDTH
    group = q_ref.shape[1] // kv_width
    rows = -(-group // 8) * 8
    span = pages * page_tokens
    scale = HEAD_WIDTH ** (-0.5)
    length = len_ref[0]
    q = q_ref[...].astype(F32)
    fk = fk_ref[...].astype(F32)
    fv = fv_ref[...].astype(F32)
    pad = [jnp.zeros((rows - group, HEAD_WIDTH), F32)] if rows > group else []
    live = lax.broadcasted_iota(jnp.int32, (rows, span), 1) < length
    blended = []
    for g in range(heads_kv):
        lanes = slice(g * HEAD_WIDTH, (g + 1) * HEAD_WIDTH)
        first = g * group
        q_g = jnp.concatenate(
            [q[:, (first + j) * HEAD_WIDTH : (first + j + 1) * HEAD_WIDTH] for j in range(group)] + pad,
            axis=0,
        )
        keys = jnp.concatenate([k_ref[table_ref[0, p], :, lanes] for p in range(pages)], axis=0)
        values = jnp.concatenate([v_ref[table_ref[0, p], :, lanes] for p in range(pages)], axis=0)
        s = (
            lax.dot_general(
                q_g.astype(BF16), keys, (((1,), (1,)), ((), ())), preferred_element_type=F32
            )
            * scale
        )
        own = jnp.sum(q_g * fk[:, lanes], axis=1, keepdims=True) * scale
        top = jnp.maximum(jnp.max(jnp.where(live, s, -jnp.inf), axis=1, keepdims=True), own)
        prob = jnp.where(live, jnp.exp(s - top), 0.0)
        own_p = jnp.exp(own - top)
        total = jnp.sum(prob, axis=1, keepdims=True) + own_p
        weights = (prob / total).astype(BF16)
        own_weight = (own_p / total).astype(BF16).astype(F32)
        out = jnp.dot(weights, values, preferred_element_type=F32) + own_weight * fv[:, lanes]
        blended.append(out[:group])
    attn = jnp.concatenate(blended, axis=0).astype(BF16)
    for r in range(o_ref.shape[0]):
        o_ref[r] = attn


def proj_kernel(attn_ref, w_ref, o_ref):
    attn = attn_ref[...].astype(F32)
    x = jnp.concatenate([attn[:, j, :] for j in range(attn.shape[1])], axis=1).astype(BF16)
    o_ref[...] = jnp.dot(x, w_ref[...], preferred_element_type=F32)


def resid_kernel(resid_ref, mine_ref, other_ref, o_ref):
    h1 = (resid_ref[...].astype(F32) + (mine_ref[...] + other_ref[...])).astype(BF16)
    for r in range(o_ref.shape[0]):
        o_ref[r] = h1


def routed_rows(routes_ref):
    count = routes_ref.shape[1]
    first = jnp.int32(count - 1)
    last = jnp.int32(0)
    for r in range(count):
        hit = jnp.logical_or(routes_ref[0, r] == 0, routes_ref[1, r] == 0)
        first = jnp.where(hit, jnp.minimum(first, r), first)
        last = jnp.where(hit, r, last)
    return first, last


def expert_kernel(
    routes_ref, h1_ref, gain_ref, router_ref, wg_ref, wu_ref, gu_ref, route_ref, own_ref,
    gu_all, route_all, own_all,
):
    units = h1_ref.shape[0]
    half = wg_ref.shape[0]
    hidden = wg_ref.shape[1]
    head = lax.axis_index("heads")
    unit = lax.axis_index("units")
    h1 = jnp.concatenate([h1_ref[u] for u in range(units)], axis=1).astype(F32)
    gain = gain_ref[...].astype(F32).reshape(1, -1)
    rstd = lax.rsqrt(jnp.mean(h1 * h1, axis=1, keepdims=True) + 1e-05)
    xn = (h1 * rstd * gain).astype(BF16)
    x_half = jnp.where(head == 0, xn[:, :half].astype(F32), xn[:, half:].astype(F32)).astype(BF16)
    own_all[...] = jnp.where(head == 0, h1[:, :half], h1[:, half:])
    own_ref[...] = own_all[pl.ds(unit, 1), :]
    gu_all[:, :hidden] = jnp.dot(x_half, wg_ref[...], preferred_element_type=F32)
    gu_all[:, hidden:] = jnp.dot(x_half, wu_ref[...], preferred_element_type=F32)
    logits = lax.dot_general(
        xn, router_ref[...], (((1,), (1,)), ((), ())), preferred_element_type=F32
    )
    expert_ids = lax.broadcasted_iota(jnp.int32, logits.shape, 1)
    row_ids = lax.broadcasted_iota(jnp.int32, (h1.shape[0], 1), 0)
    one = jnp.zeros(row_ids.shape, jnp.int32)
    two = jnp.zeros(row_ids.shape, jnp.int32)
    for r in range(h1.shape[0]):
        one = jnp.where(row_ids == r, routes_ref[0, r], one)
        two = jnp.where(row_ids == r, routes_ref[1, r], two)
    chosen_one = jnp.sum(jnp.where(expert_ids == one, logits, 0.0), axis=1, keepdims=True)
    chosen_two = jnp.sum(jnp.where(expert_ids == two, logits, 0.0), axis=1, keepdims=True)
    diff = jnp.where(one == 0, chosen_one - chosen_two, chosen_two - chosen_one)
    route = jnp.where(jnp.logical_or(one == 0, two == 0), 1.0 / (1.0 + jnp.exp(-diff)), 0.0)
    route_all[...] = jnp.broadcast_to(route, route_all.shape)
    for slot, r in enumerate(routed_rows(routes_ref)):
        gu_ref[slot : slot + 1, :] = gu_all[pl.ds(r, 1), :]
        route_ref[slot : slot + 1, :] = route_all[pl.ds(r, 1), :]


def down_kernel(routes_ref, mine_ref, other_ref, route_ref, wd_ref, o_ref):
    hidden = wd_ref.shape[0]
    gu = mine_ref[...] + other_ref[...]
    gate = gu[:, :hidden]
    up = gu[:, hidden:]
    act = (gate / (1.0 + jnp.exp(-gate)) * up * route_ref[:, 0:1]).astype(BF16)
    full = jnp.dot(act, wd_ref[...], preferred_element_type=F32)
    o_ref[...] = jnp.zeros(o_ref.shape, F32)
    for slot, r in enumerate(routed_rows(routes_ref)):
        for j in range(o_ref.shape[1]):
            o_ref[r, j : j + 1, :] = full[slot : slot + 1, j * LANES : (j + 1) * LANES]


def sum_kernel(parts_ref, own_ref, o_ref):
    moe = parts_ref[0]
    for u in range(1, parts_ref.shape[0]):
        moe = moe + parts_ref[u]
    for j in range(parts_ref.shape[1]):
        lanes = slice(j * LANES, (j + 1) * LANES)
        o_ref[:, lanes] = (own_ref[:, lanes] + moe[j : j + 1, :]).astype(o_ref.dtype)


SMEM = pl.BlockSpec(memory_space=pltpu.SMEM)
VMEM = pl.BlockSpec(memory_space=pltpu.VMEM)
ANY = pl.BlockSpec(memory_space=pltpu.HBM)


def in_hbm(x):
    return pltpu.with_memory_space_constraint(x, pltpu.HBM)


def in_vmem(x):
    return pltpu.with_memory_space_constraint(x, pltpu.VMEM)


def small_body(
    queries,
    fresh_key,
    fresh_value,
    key_cache_pages,
    value_cache_pages,
    page_table,
    lengths,
    resid,
    w_out,
    norm_gain,
    router,
    routes,
    w_gate,
    w_up,
    w_down,
):
    rows = routes.shape[0]
    half = w_gate.shape[0]
    chunks = half // LANES
    hidden = w_gate.shape[1]
    cols = w_out.shape[1]
    swap = [(0, 1), (1, 0)]
    routes_t = routes.T

    def exchange(x):
        return lax.all_to_all(x, "units", split_axis=0, concat_axis=0, tiled=True)

    def call(kernel, out, specs, name, scratch=(), limit=6, more=()):
        more = [in_hbm(w) for w in more]

        def whole(*refs):
            n = len(specs)
            kernel(*refs[:n], *refs[n + len(more):])

        f = pl.pallas_call(
            whole,
            out_shape=out,
            in_specs=specs + [ANY] * len(more),
            out_specs=jax.tree.map(lambda _: VMEM, out),
            scratch_shapes=scratch,
            compiler_params=pltpu.CompilerParams(vmem_limit_bytes=limit * MIB),
            name=name,
        )
        return lambda *ops: f(*ops, *more)

    attn = call(
        attn_kernel,
        jax.ShapeDtypeStruct((rows, chunks, LANES), BF16),
        [SMEM] + [ANY] * 6,
        "attend",
        scratch=(
            pltpu.SMEM(page_table.shape, page_table.dtype),
            *(
                pltpu.VMEM(x.shape, x.dtype)
                for x in (queries, fresh_key, fresh_value, key_cache_pages, value_cache_pages)
            ),
            pltpu.SemaphoreType.DMA((6,)),
        ),
        more=(w_gate, w_up, w_down),
    )(
        lengths,
        *map(in_hbm, (page_table, queries, fresh_key, fresh_value, key_cache_pages, value_cache_pages)),
    )
    attn_all = exchange(attn)
    proj = call(proj_kernel, jax.ShapeDtypeStruct((rows, cols), F32), [VMEM] * 2, "proj")(
        attn_all, in_vmem(w_out)
    )
    proj_other = lax.ppermute(proj, "heads", swap)
    h1_cols = call(
        resid_kernel, jax.ShapeDtypeStruct((rows, rows, cols), BF16), [VMEM] * 3, "resid"
    )(resid, proj, proj_other)
    h1 = exchange(h1_cols)
    gu, route, own_h1 = call(
        expert_kernel,
        (
            jax.ShapeDtypeStruct((2, 2 * hidden), F32),
            jax.ShapeDtypeStruct((2, LANES), F32),
            jax.ShapeDtypeStruct((1, half), F32),
        ),
        [SMEM] + [VMEM] * 5,
        "expert",
        scratch=(
            pltpu.VMEM((rows, 2 * hidden), F32),
            pltpu.VMEM((rows, LANES), F32),
            pltpu.VMEM((rows, half), F32),
        ),
    )(
        routes_t, h1, norm_gain, router.T, in_vmem(w_gate), in_vmem(w_up)
    )
    gu_other = lax.ppermute(gu, "heads", swap)
    full = call(
        down_kernel,
        jax.ShapeDtypeStruct((rows, chunks, LANES), F32),
        [SMEM] + [VMEM] * 4,
        "down",
    )(routes_t, gu, gu_other, route, in_vmem(w_down))
    parts = exchange(full)
    return call(sum_kernel, jax.ShapeDtypeStruct((1, half), BF16), [VMEM] * 2, "total")(
        parts, own_h1
    )


def one_tile(*args):
    queries, routes, router = args[0], args[11], args[10]
    rows = routes.shape[0]
    units = lax.axis_size("units")
    return (
        queries.shape[0] == 1
        and rows == 8
        and units == rows
        and rows * routes.shape[1] // router.shape[1] == 2
    )


def dispatch(*args):
    return small_body(*args) if one_tile(*args) else body(*args)


def solution(mesh):
    in_specs = (
        P(("groups", "units"), "heads"),
        P(("groups", "units"), "heads"),
        P(("groups", "units"), "heads"),
        P(("groups", "units"), None, "heads"),
        P(("groups", "units"), None, "heads"),
        P(("groups", "units"), None),
        P(("groups", "units")),
        P("groups", "units"),
        P("heads", "units"),
        P(),
        P(),
        P("groups", None),
        P("heads", "units"),
        P("heads", "units"),
        P("units", "heads"),
    )
    out_specs = P(("groups", "units"), "heads")
    return jax.shard_map(dispatch, mesh=mesh, in_specs=in_specs, out_specs=out_specs, check_vma=False)
```

```python
import functools

import jax
import jax.numpy as jnp
from jax import lax
from jax.experimental import pallas as pl
from jax.experimental.pallas import tpu as pltpu
from jax.sharding import PartitionSpec as P

HEAD_WIDTH = 128
LANES = 128
F32 = jnp.float32
BF16 = jnp.bfloat16
MIB = 2**20


def attend(
    queries, fresh_key, fresh_value, key_cache_pages, value_cache_pages, page_table, lengths
):
    token_rows = queries.shape[0]
    kv_width = fresh_key.shape[1]
    heads_kv = kv_width // HEAD_WIDTH
    query_group = queries.shape[1] // kv_width
    score_scale = HEAD_WIDTH ** (-0.5)
    key_rows = key_cache_pages[page_table].reshape(token_rows, -1, heads_kv, HEAD_WIDTH)
    value_rows = value_cache_pages[page_table].reshape(token_rows, -1, heads_kv, HEAD_WIDTH)
    query_grid = queries.reshape(token_rows, heads_kv, query_group, HEAD_WIDTH)
    scores = (
        jnp.einsum("rgjd,rtgd->rgjt", query_grid, key_rows, preferred_element_type=jnp.float32)
        * score_scale
    )
    expert_owned = (
        jnp.einsum(
            "fiam,fim->fia",
            query_grid,
            fresh_key.reshape(token_rows, heads_kv, HEAD_WIDTH),
            preferred_element_type=jnp.float32,
        )
        * score_scale
    )
    span = key_rows.shape[1]
    live = (jnp.arange(span, dtype=jnp.int32)[None, :] < lengths[:, None])[:, None, None, :]
    top = jnp.maximum(jnp.max(jnp.where(live, scores, -jnp.inf), axis=-1), expert_owned)
    prob = jnp.where(live, jnp.exp(scores - top[..., None]), 0.0)
    own_p = jnp.exp(expert_owned - top)
    total = jnp.sum(prob, axis=-1) + own_p
    weights = (prob / total[..., None]).astype(jnp.bfloat16)
    owned_weight = (own_p / total).astype(jnp.bfloat16)
    blended_values = jnp.einsum(
        "rgjt,rtgd->rgjd", weights, value_rows, preferred_element_type=jnp.float32
    )
    blended_values = blended_values + owned_weight.astype(jnp.float32)[
        ..., None
    ] * fresh_value.reshape(token_rows, heads_kv, 1, HEAD_WIDTH).astype(jnp.float32)
    return blended_values.reshape(token_rows, -1).astype(jnp.bfloat16)


def route_weight(logits, routes):
    picks = (
        routes[:, :, None] == jnp.arange(logits.shape[1], dtype=jnp.int32)[None, None, :]
    ).astype(jnp.float32)
    chosen = jnp.sum(picks * logits[:, None, :], axis=-1)
    first = jax.nn.sigmoid(chosen[:, 0] - chosen[:, 1])
    second = jax.nn.sigmoid(chosen[:, 1] - chosen[:, 0])
    return jnp.where(routes[:, 0] == 0, first, jnp.where(routes[:, 1] == 0, second, 0.0))


def body(
    queries,
    fresh_key,
    fresh_value,
    key_cache_pages,
    value_cache_pages,
    page_table,
    lengths,
    resid,
    w_out,
    norm_gain,
    router,
    routes,
    w_gate,
    w_up,
    w_down,
):
    own_rows = queries.shape[0]
    half_width = w_gate.shape[0]
    all_rows = routes.shape[0]
    routed_count = all_rows * routes.shape[1] // router.shape[1]
    unit_index = lax.axis_index("units")
    head_index = lax.axis_index("heads")
    attn = attend(
        queries, fresh_key, fresh_value, key_cache_pages, value_cache_pages, page_table, lengths
    )
    proj_part = jnp.dot(
        lax.all_gather(attn, "units", axis=0, tiled=True), w_out, preferred_element_type=jnp.float32
    )
    proj = lax.psum(proj_part, "heads")
    h1_cols = (resid.astype(jnp.float32) + proj).astype(jnp.bfloat16)
    h1 = lax.all_gather(h1_cols, "units", axis=1, tiled=True)
    is_routed = jnp.any(routes == 0, axis=1)
    slot_of = jnp.cumsum(is_routed.astype(jnp.int32)) - 1
    slot_ids = jnp.arange(routed_count, dtype=jnp.int32)
    row_ids = jnp.arange(all_rows, dtype=jnp.int32)
    match = (slot_of[None, :] == slot_ids[:, None]) & is_routed[None, :]
    picked_rows = jnp.sum(jnp.where(match, row_ids[None, :], 0), axis=1)
    h1_sel = h1[picked_rows]
    hf_sel = h1_sel.astype(jnp.float32)
    rstd = lax.rsqrt(jnp.mean(hf_sel * hf_sel, axis=-1, keepdims=True) + 1e-05)
    xn_sel = (hf_sel * rstd * norm_gain.astype(jnp.float32)).astype(jnp.bfloat16)
    logits = jnp.dot(xn_sel, router, preferred_element_type=jnp.float32)
    route = route_weight(logits, routes[picked_rows])
    xn_half = lax.dynamic_slice_in_dim(xn_sel, head_index * half_width, half_width, 1)
    gate_part = jnp.dot(xn_half, w_gate, preferred_element_type=jnp.float32)
    up_part = jnp.dot(xn_half, w_up, preferred_element_type=jnp.float32)
    gate, up = lax.psum((gate_part, up_part), "heads")
    hidden = (jax.nn.silu(gate) * up * route[:, None]).astype(jnp.bfloat16)
    full_term = jnp.dot(hidden, w_down, preferred_element_type=jnp.float32)
    own_start = unit_index * own_rows
    own_h1 = lax.dynamic_slice_in_dim(
        lax.dynamic_slice_in_dim(h1, own_start, own_rows, 0), head_index * half_width, half_width, 1
    )
    own_routed = lax.dynamic_slice_in_dim(is_routed, own_start, own_rows, 0)
    own_slot = jnp.maximum(lax.dynamic_slice_in_dim(slot_of, own_start, own_rows, 0), 0)
    moe_sel = lax.psum(full_term, "units")
    moe_own = jnp.where(own_routed[:, None], moe_sel[own_slot], 0.0)
    return (own_h1.astype(jnp.float32) + moe_own).astype(jnp.bfloat16)


def attn_kernel(
    len_ref, table_hbm, q_hbm, fk_hbm, fv_hbm, k_hbm, v_hbm, o_ref,
    table_ref, q_ref, fk_ref, fv_ref, k_ref, v_ref, sems,
):
    pairs = {
        "q": (q_hbm, q_ref),
        "fk": (fk_hbm, fk_ref),
        "table": (table_hbm, table_ref),
        "k": (k_hbm, k_ref),
        "v": (v_hbm, v_ref),
        "fv": (fv_hbm, fv_ref),
    }
    copies = {
        name: pltpu.make_async_copy(src, dst, sems.at[i]) for i, (name, (src, dst)) in enumerate(pairs.items())
    }
    for copy in copies.values():
        copy.start()
    pages, page_tokens, kv_width = k_ref.shape
    heads_kv = kv_width // HEAD_WIDTH
    group = q_ref.shape[1] // kv_width
    rows = -(-group // 8) * 8
    span = pages * page_tokens
    scale = HEAD_WIDTH ** (-0.5)
    length = len_ref[0]
    pad = [jnp.zeros((rows - group, HEAD_WIDTH), F32)] if rows > group else []
    live = lax.broadcasted_iota(jnp.int32, (rows, span), 1) < length
    heads = [slice(g * HEAD_WIDTH, (g + 1) * HEAD_WIDTH) for g in range(heads_kv)]
    copies["q"].wait()
    copies["fk"].wait()
    q = q_ref[...].astype(F32)
    fk = fk_ref[...].astype(F32)
    q_grid = [
        jnp.concatenate(
            [q[:, (g * group + j) * HEAD_WIDTH : (g * group + j + 1) * HEAD_WIDTH] for j in range(group)] + pad,
            axis=0,
        )
        for g in range(heads_kv)
    ]
    owns = [
        jnp.sum(q_g * fk[:, lanes], axis=1, keepdims=True) * scale for q_g, lanes in zip(q_grid, heads)
    ]
    q_grid = [q_g.astype(BF16) for q_g in q_grid]
    copies["table"].wait()
    copies["k"].wait()
    table = [table_ref[0, p] for p in range(pages)]
    scores = [
        lax.dot_general(
            q_g,
            jnp.concatenate([k_ref[page, :, lanes] for page in table], axis=0),
            (((1,), (1,)), ((), ())),
            preferred_element_type=F32,
        )
        * scale
        for q_g, lanes in zip(q_grid, heads)
    ]
    weights, own_weights = [], []
    for s, own in zip(scores, owns):
        top = jnp.maximum(jnp.max(jnp.where(live, s, -jnp.inf), axis=1, keepdims=True), own)
        prob = jnp.where(live, jnp.exp(s - top), 0.0)
        own_p = jnp.exp(own - top)
        total = jnp.sum(prob, axis=1, keepdims=True) + own_p
        weights.append((prob / total).astype(BF16))
        own_weights.append((own_p / total).astype(BF16).astype(F32))
    copies["v"].wait()
    copies["fv"].wait()
    fv = fv_ref[...].astype(F32)
    blended = [
        (
            jnp.dot(
                w,
                jnp.concatenate([v_ref[page, :, lanes] for page in table], axis=0),
                preferred_element_type=F32,
            )
            + own_w * fv[:, lanes]
        )[:group]
        for w, own_w, lanes in zip(weights, own_weights, heads)
    ]
    attn = jnp.concatenate(blended, axis=0).astype(BF16)
    for r in range(o_ref.shape[0]):
        o_ref[r] = attn


def proj_kernel(attn_ref, w_ref, o_ref):
    attn = attn_ref[...].astype(F32)
    x = jnp.concatenate([attn[:, j, :] for j in range(attn.shape[1])], axis=1).astype(BF16)
    o_ref[...] = jnp.dot(x, w_ref[...], preferred_element_type=F32)


def resid_kernel(resid_ref, mine_ref, other_ref, o_ref):
    h1 = (resid_ref[...].astype(F32) + (mine_ref[...] + other_ref[...])).astype(BF16)
    for r in range(o_ref.shape[0]):
        o_ref[r] = h1


def routed_rows(routes_ref):
    count = routes_ref.shape[1]
    first = jnp.int32(count - 1)
    last = jnp.int32(0)
    for r in range(count):
        hit = jnp.logical_or(routes_ref[0, r] == 0, routes_ref[1, r] == 0)
        first = jnp.where(hit, jnp.minimum(first, r), first)
        last = jnp.where(hit, r, last)
    return first, last


def expert_kernel(routes_ref, h1_ref, gain_ref, wg_ref, wu_ref, gu_ref, gu_all):
    units, _, cols = h1_ref.shape
    hidden = wg_ref.shape[1]
    per_half = units // 2
    head = lax.axis_index("heads")
    half = per_half * cols
    gain = gain_ref[...].astype(F32).reshape(1, -1)
    gain = jnp.where(head == 0, gain[:, :half], gain[:, half:])
    h1 = jnp.concatenate([h1_ref[head * per_half + i] for i in range(per_half)], axis=1).astype(F32)
    x = (h1 * gain).astype(BF16)
    gu_all[:, :hidden] = jnp.dot(x, wg_ref[...], preferred_element_type=F32)
    gu_all[:, hidden:] = jnp.dot(x, wu_ref[...], preferred_element_type=F32)
    for slot, r in enumerate(routed_rows(routes_ref)):
        gu_ref[slot : slot + 1, :] = gu_all[pl.ds(r, 1), :]


def side_kernel(routes_ref, h1_ref, gain_ref, router_ref, stat_ref, own_ref, h_all, router_all):
    units, _, cols = h1_ref.shape
    per_half = units // 2
    head = lax.axis_index("heads")
    unit = lax.axis_index("units")
    for u in range(units):
        h_all[:, u * cols : (u + 1) * cols] = h1_ref[u].astype(F32)
    own = h_all[pl.ds(unit, 1), :]
    half = per_half * cols
    own_ref[...] = jnp.where(head == 0, own[:, :half], own[:, half:])
    router_all[...] = router_ref[...].astype(F32)
    gain = gain_ref[...].astype(F32).reshape(1, -1)
    for slot, r in enumerate(routed_rows(routes_ref)):
        h = h_all[pl.ds(r, 1), :]
        rstd = lax.rsqrt(jnp.mean(h * h, axis=1, keepdims=True) + 1e-05)
        xn = (h * rstd * gain).astype(BF16).astype(F32)
        other = jnp.where(routes_ref[0, r] == 0, routes_ref[1, r], routes_ref[0, r])
        diff = jnp.sum(xn * router_all[0:1, :], axis=1, keepdims=True) - jnp.sum(
            xn * router_all[pl.ds(other, 1), :], axis=1, keepdims=True
        )
        route = 1.0 / (1.0 + jnp.exp(-diff))
        lane_ids = lax.broadcasted_iota(jnp.int32, (1, LANES), 1)
        stat_ref[slot : slot + 1, :] = jnp.where(lane_ids == 0, rstd, route)


def down_kernel(routes_ref, mine_ref, other_ref, stat_ref, wd_ref, o16_ref, o_ref):
    hidden = wd_ref.shape[0]
    rstd = stat_ref[:, 0:1]
    route = stat_ref[:, 1:2]
    gate = (mine_ref[:, :hidden] + other_ref[:, :hidden]) * rstd
    up = (mine_ref[:, hidden:] + other_ref[:, hidden:]) * (rstd * route)
    act = (gate / (1.0 + jnp.exp(-gate)) * up).astype(BF16)
    full = jnp.dot(act, wd_ref[...], preferred_element_type=F32)
    o_ref[...] = jnp.zeros(o_ref.shape, F32)
    for slot, r in enumerate(routed_rows(routes_ref)):
        for j in range(o_ref.shape[1]):
            o_ref[r, j : j + 1, :] = full[slot : slot + 1, j * LANES : (j + 1) * LANES]
    o16_ref[...] = o_ref[...].astype(BF16)


def sum_kernel(parts_ref, own_ref, o_ref):
    moe = parts_ref[0].astype(F32)
    for u in range(1, parts_ref.shape[0]):
        moe = moe + parts_ref[u].astype(F32)
    for j in range(parts_ref.shape[1]):
        lanes = slice(j * LANES, (j + 1) * LANES)
        o_ref[:, lanes] = (own_ref[:, lanes] + moe[j : j + 1, :]).astype(o_ref.dtype)


SMEM = pl.BlockSpec(memory_space=pltpu.SMEM)
VMEM = pl.BlockSpec(memory_space=pltpu.VMEM)
ANY = pl.BlockSpec(memory_space=pltpu.HBM)


def in_hbm(x):
    return pltpu.with_memory_space_constraint(x, pltpu.HBM)


def in_vmem(x):
    return pltpu.with_memory_space_constraint(x, pltpu.VMEM)


def small_body(
    queries,
    fresh_key,
    fresh_value,
    key_cache_pages,
    value_cache_pages,
    page_table,
    lengths,
    resid,
    w_out,
    norm_gain,
    router,
    routes,
    w_gate,
    w_up,
    w_down,
):
    rows = routes.shape[0]
    half = w_gate.shape[0]
    chunks = half // LANES
    hidden = w_gate.shape[1]
    cols = w_out.shape[1]
    swap = [(0, 1), (1, 0)]
    routes_t = routes.T

    def exchange(x):
        return lax.all_to_all(x, "units", split_axis=0, concat_axis=0, tiled=True)

    def call(kernel, out, specs, name, scratch=(), limit=6, more=()):
        more = [in_hbm(w) for w in more]

        def whole(*refs):
            n = len(specs)
            kernel(*refs[:n], *refs[n + len(more):])

        f = pl.pallas_call(
            whole,
            out_shape=out,
            in_specs=specs + [ANY] * len(more),
            out_specs=jax.tree.map(lambda _: VMEM, out),
            scratch_shapes=scratch,
            compiler_params=pltpu.CompilerParams(vmem_limit_bytes=limit * MIB),
            name=name,
        )
        return lambda *ops: f(*ops, *more)

    attn = call(
        attn_kernel,
        jax.ShapeDtypeStruct((rows, chunks, LANES), BF16),
        [SMEM] + [ANY] * 6,
        "attend",
        scratch=(
            pltpu.SMEM(page_table.shape, page_table.dtype),
            *(
                pltpu.VMEM(x.shape, x.dtype)
                for x in (queries, fresh_key, fresh_value, key_cache_pages, value_cache_pages)
            ),
            pltpu.SemaphoreType.DMA((6,)),
        ),
        more=(w_gate, w_up, w_down),
    )(
        lengths,
        *map(in_hbm, (page_table, queries, fresh_key, fresh_value, key_cache_pages, value_cache_pages)),
    )
    attn_all = exchange(attn)
    proj = call(proj_kernel, jax.ShapeDtypeStruct((rows, cols), F32), [VMEM] * 2, "proj")(
        attn_all, in_vmem(w_out)
    )
    proj_other = lax.ppermute(proj, "heads", swap)
    h1_cols = call(
        resid_kernel, jax.ShapeDtypeStruct((rows, rows, cols), BF16), [VMEM] * 3, "resid"
    )(resid, proj, proj_other)
    h1 = exchange(h1_cols)
    gu = call(
        expert_kernel,
        jax.ShapeDtypeStruct((2, 2 * hidden), F32),
        [SMEM] + [VMEM] * 4,
        "expert",
        scratch=(pltpu.VMEM((rows, 2 * hidden), F32),),
    )(routes_t, h1, norm_gain, in_vmem(w_gate), in_vmem(w_up))
    gu_other = lax.ppermute(gu, "heads", swap)
    stat, own_h1 = call(
        side_kernel,
        (jax.ShapeDtypeStruct((2, LANES), F32), jax.ShapeDtypeStruct((1, half), F32)),
        [SMEM] + [VMEM] * 3,
        "side",
        scratch=(pltpu.VMEM((rows, 2 * half), F32), pltpu.VMEM(router.shape[::-1], F32)),
    )(routes_t, h1, norm_gain, router.T)
    full = call(
        down_kernel,
        jax.ShapeDtypeStruct((rows, chunks, LANES), BF16),
        [SMEM] + [VMEM] * 4,
        "down",
        scratch=(pltpu.VMEM((rows, chunks, LANES), F32),),
    )(routes_t, gu, gu_other, stat, in_vmem(w_down))
    parts = exchange(full)
    return call(sum_kernel, jax.ShapeDtypeStruct((1, half), BF16), [VMEM] * 2, "total")(
        parts, own_h1
    )


def one_tile(*args):
    queries, routes, router = args[0], args[11], args[10]
    rows = routes.shape[0]
    units = lax.axis_size("units")
    return (
        queries.shape[0] == 1
        and rows == 8
        and units == rows
        and rows * routes.shape[1] // router.shape[1] == 2
    )


def dispatch(*args):
    return small_body(*args) if one_tile(*args) else body(*args)


def solution(mesh):
    in_specs = (
        P(("groups", "units"), "heads"),
        P(("groups", "units"), "heads"),
        P(("groups", "units"), "heads"),
        P(("groups", "units"), None, "heads"),
        P(("groups", "units"), None, "heads"),
        P(("groups", "units"), None),
        P(("groups", "units")),
        P("groups", "units"),
        P("heads", "units"),
        P(),
        P(),
        P("groups", None),
        P("heads", "units"),
        P("heads", "units"),
        P("units", "heads"),
    )
    out_specs = P(("groups", "units"), "heads")
    return jax.shard_map(dispatch, mesh=mesh, in_specs=in_specs, out_specs=out_specs, check_vma=False)
```

```python
import functools

import jax
import jax.numpy as jnp
from jax import lax
from jax.experimental import pallas as pl
from jax.experimental.pallas import tpu as pltpu
from jax.sharding import PartitionSpec as P

HEAD_WIDTH = 128
LANES = 128
F32 = jnp.float32
BF16 = jnp.bfloat16
MIB = 2**20


def attend(
    queries, fresh_key, fresh_value, key_cache_pages, value_cache_pages, page_table, lengths
):
    token_rows = queries.shape[0]
    kv_width = fresh_key.shape[1]
    heads_kv = kv_width // HEAD_WIDTH
    query_group = queries.shape[1] // kv_width
    score_scale = HEAD_WIDTH ** (-0.5)
    key_rows = key_cache_pages[page_table].reshape(token_rows, -1, heads_kv, HEAD_WIDTH)
    value_rows = value_cache_pages[page_table].reshape(token_rows, -1, heads_kv, HEAD_WIDTH)
    query_grid = queries.reshape(token_rows, heads_kv, query_group, HEAD_WIDTH)
    scores = (
        jnp.einsum("rgjd,rtgd->rgjt", query_grid, key_rows, preferred_element_type=jnp.float32)
        * score_scale
    )
    expert_owned = (
        jnp.einsum(
            "fiam,fim->fia",
            query_grid,
            fresh_key.reshape(token_rows, heads_kv, HEAD_WIDTH),
            preferred_element_type=jnp.float32,
        )
        * score_scale
    )
    span = key_rows.shape[1]
    live = (jnp.arange(span, dtype=jnp.int32)[None, :] < lengths[:, None])[:, None, None, :]
    top = jnp.maximum(jnp.max(jnp.where(live, scores, -jnp.inf), axis=-1), expert_owned)
    prob = jnp.where(live, jnp.exp(scores - top[..., None]), 0.0)
    own_p = jnp.exp(expert_owned - top)
    total = jnp.sum(prob, axis=-1) + own_p
    weights = (prob / total[..., None]).astype(jnp.bfloat16)
    owned_weight = (own_p / total).astype(jnp.bfloat16)
    blended_values = jnp.einsum(
        "rgjt,rtgd->rgjd", weights, value_rows, preferred_element_type=jnp.float32
    )
    blended_values = blended_values + owned_weight.astype(jnp.float32)[
        ..., None
    ] * fresh_value.reshape(token_rows, heads_kv, 1, HEAD_WIDTH).astype(jnp.float32)
    return blended_values.reshape(token_rows, -1).astype(jnp.bfloat16)


def route_weight(logits, routes):
    picks = (
        routes[:, :, None] == jnp.arange(logits.shape[1], dtype=jnp.int32)[None, None, :]
    ).astype(jnp.float32)
    chosen = jnp.sum(picks * logits[:, None, :], axis=-1)
    first = jax.nn.sigmoid(chosen[:, 0] - chosen[:, 1])
    second = jax.nn.sigmoid(chosen[:, 1] - chosen[:, 0])
    return jnp.where(routes[:, 0] == 0, first, jnp.where(routes[:, 1] == 0, second, 0.0))


def body(
    queries,
    fresh_key,
    fresh_value,
    key_cache_pages,
    value_cache_pages,
    page_table,
    lengths,
    resid,
    w_out,
    norm_gain,
    router,
    routes,
    w_gate,
    w_up,
    w_down,
):
    own_rows = queries.shape[0]
    half_width = w_gate.shape[0]
    all_rows = routes.shape[0]
    routed_count = all_rows * routes.shape[1] // router.shape[1]
    unit_index = lax.axis_index("units")
    head_index = lax.axis_index("heads")
    attn = attend(
        queries, fresh_key, fresh_value, key_cache_pages, value_cache_pages, page_table, lengths
    )
    proj_part = jnp.dot(
        lax.all_gather(attn, "units", axis=0, tiled=True), w_out, preferred_element_type=jnp.float32
    )
    proj = lax.psum(proj_part, "heads")
    h1_cols = (resid.astype(jnp.float32) + proj).astype(jnp.bfloat16)
    h1 = lax.all_gather(h1_cols, "units", axis=1, tiled=True)
    is_routed = jnp.any(routes == 0, axis=1)
    slot_of = jnp.cumsum(is_routed.astype(jnp.int32)) - 1
    slot_ids = jnp.arange(routed_count, dtype=jnp.int32)
    row_ids = jnp.arange(all_rows, dtype=jnp.int32)
    match = (slot_of[None, :] == slot_ids[:, None]) & is_routed[None, :]
    picked_rows = jnp.sum(jnp.where(match, row_ids[None, :], 0), axis=1)
    h1_sel = h1[picked_rows]
    hf_sel = h1_sel.astype(jnp.float32)
    rstd = lax.rsqrt(jnp.mean(hf_sel * hf_sel, axis=-1, keepdims=True) + 1e-05)
    xn_sel = (hf_sel * rstd * norm_gain.astype(jnp.float32)).astype(jnp.bfloat16)
    logits = jnp.dot(xn_sel, router, preferred_element_type=jnp.float32)
    route = route_weight(logits, routes[picked_rows])
    xn_half = lax.dynamic_slice_in_dim(xn_sel, head_index * half_width, half_width, 1)
    gate_part = jnp.dot(xn_half, w_gate, preferred_element_type=jnp.float32)
    up_part = jnp.dot(xn_half, w_up, preferred_element_type=jnp.float32)
    gate, up = lax.psum((gate_part, up_part), "heads")
    hidden = (jax.nn.silu(gate) * up * route[:, None]).astype(jnp.bfloat16)
    full_term = jnp.dot(hidden, w_down, preferred_element_type=jnp.float32)
    own_start = unit_index * own_rows
    own_h1 = lax.dynamic_slice_in_dim(
        lax.dynamic_slice_in_dim(h1, own_start, own_rows, 0), head_index * half_width, half_width, 1
    )
    own_routed = lax.dynamic_slice_in_dim(is_routed, own_start, own_rows, 0)
    own_slot = jnp.maximum(lax.dynamic_slice_in_dim(slot_of, own_start, own_rows, 0), 0)
    moe_sel = lax.psum(full_term, "units")
    moe_own = jnp.where(own_routed[:, None], moe_sel[own_slot], 0.0)
    return (own_h1.astype(jnp.float32) + moe_own).astype(jnp.bfloat16)


def begin_kernel(o_ref):
    o_ref[...] = jnp.zeros(o_ref.shape, F32)


def attn_kernel(begun_ref, len_ref, table_ref, q_ref, fk_ref, fv_ref, k_ref, v_ref, o_ref):
    pages, page_tokens, kv_width = k_ref.shape
    heads_kv = kv_width // HEAD_WIDTH
    group = q_ref.shape[1] // kv_width
    rows = -(-group // 8) * 8
    scale = HEAD_WIDTH ** (-0.5)
    length = len_ref[0]
    pad = [jnp.zeros((rows - group, HEAD_WIDTH), F32)] if rows > group else []
    table = table_ref[...]
    slots = lax.broadcasted_iota(jnp.int32, table.shape, 1)
    tokens = lax.broadcasted_iota(jnp.int32, (rows, page_tokens), 1)
    live = jnp.concatenate(
        [
            tokens + page_tokens * jnp.sum(jnp.where(table == page, slots, 0), axis=1, keepdims=True) < length
            for page in range(pages)
        ],
        axis=1,
    )
    heads = [slice(g * HEAD_WIDTH, (g + 1) * HEAD_WIDTH) for g in range(heads_kv)]
    q = q_ref[...].astype(F32)
    fk = fk_ref[...].astype(F32)
    q_grid = [
        jnp.concatenate(
            [q[:, (g * group + j) * HEAD_WIDTH : (g * group + j + 1) * HEAD_WIDTH] for j in range(group)] + pad,
            axis=0,
        )
        for g in range(heads_kv)
    ]
    owns = [
        jnp.sum(q_g * fk[:, lanes], axis=1, keepdims=True) * scale for q_g, lanes in zip(q_grid, heads)
    ]
    q_grid = [q_g.astype(BF16) for q_g in q_grid]
    scores = [
        lax.dot_general(
            q_g,
            jnp.concatenate([k_ref[page, :, lanes] for page in range(pages)], axis=0),
            (((1,), (1,)), ((), ())),
            preferred_element_type=F32,
        )
        * scale
        for q_g, lanes in zip(q_grid, heads)
    ]
    weights, own_weights = [], []
    for s, own in zip(scores, owns):
        top = jnp.maximum(jnp.max(jnp.where(live, s, -jnp.inf), axis=1, keepdims=True), own)
        prob = jnp.where(live, jnp.exp(s - top), 0.0)
        own_p = jnp.exp(own - top)
        total = jnp.sum(prob, axis=1, keepdims=True) + own_p
        weights.append((prob / total).astype(BF16))
        own_weights.append((own_p / total).astype(BF16).astype(F32))
    fv = fv_ref[...].astype(F32)
    blended = [
        (
            jnp.dot(
                w,
                jnp.concatenate([v_ref[page, :, lanes] for page in range(pages)], axis=0),
                preferred_element_type=F32,
            )
            + own_w * fv[:, lanes]
        )[:group]
        for w, own_w, lanes in zip(weights, own_weights, heads)
    ]
    attn = jnp.concatenate(blended, axis=0).astype(BF16)
    for r in range(o_ref.shape[0]):
        o_ref[r] = attn


def proj_kernel(attn_ref, w_ref, routes_ref, o_ref, slot_ref):
    attn = attn_ref[...].astype(F32)
    x = jnp.concatenate([attn[:, j, :] for j in range(attn.shape[1])], axis=1).astype(BF16)
    o_ref[...] = jnp.dot(x, w_ref[...], preferred_element_type=F32)
    hit = jnp.logical_or(routes_ref[0:1, :] == 0, routes_ref[1:2, :] == 0)
    ids = lax.broadcasted_iota(jnp.int32, hit.shape, 1)
    first = jnp.min(jnp.where(hit, ids, hit.shape[1]), axis=1, keepdims=True)
    last = jnp.max(jnp.where(hit, ids, -1), axis=1, keepdims=True)
    request = lax.broadcasted_iota(jnp.int32, slot_ref.shape, 0)
    lane = lax.broadcasted_iota(jnp.int32, slot_ref.shape, 1)
    chosen = jnp.where(lane == 0, first, jnp.where(lane == 1, last, -1))
    slot_ref[...] = jnp.where(request == chosen, 1.0, 0.0)


def resid_kernel(resid_ref, mine_ref, other_ref, slot_ref, o_ref):
    h1 = (resid_ref[...].astype(F32) + (mine_ref[...] + other_ref[...])).astype(BF16).astype(F32)
    routed = [
        jnp.sum(jnp.where(slot_ref[:, s : s + 1] > 0.0, h1, 0.0), axis=0, keepdims=True) for s in range(2)
    ]
    for r in range(o_ref.shape[0]):
        own = h1[r : r + 1]
        o_ref[r] = jnp.concatenate(routed + [own, own], axis=0).astype(BF16)


def routed_rows(routes_ref):
    count = routes_ref.shape[1]
    first = jnp.int32(count - 1)
    last = jnp.int32(0)
    for r in range(count):
        hit = jnp.logical_or(routes_ref[0, r] == 0, routes_ref[1, r] == 0)
        first = jnp.where(hit, jnp.minimum(first, r), first)
        last = jnp.where(hit, r, last)
    return first, last


def expert_kernel(h1_ref, gain_ref, wg_ref, wu_ref, gu_ref):
    units, _, cols = h1_ref.shape
    hidden = wg_ref.shape[1]
    per_half = units // 2
    head = lax.axis_index("heads")
    half = per_half * cols
    gain = gain_ref[...].astype(F32).reshape(1, -1)
    gain = jnp.where(head == 0, gain[:, :half], gain[:, half:])
    h1 = jnp.concatenate([h1_ref[head * per_half + i].astype(F32)[:2] for i in range(per_half)], axis=1)
    x = (h1 * gain).astype(BF16)
    gu_ref[:, :hidden] = jnp.dot(x, wg_ref[...], preferred_element_type=F32)
    gu_ref[:, hidden:] = jnp.dot(x, wu_ref[...], preferred_element_type=F32)


def side_kernel(routes_ref, h1_ref, gain_ref, router_ref, stat_ref, own_ref, router_all):
    units, _, cols = h1_ref.shape
    per_half = units // 2
    head = lax.axis_index("heads")
    for i in range(per_half):
        own_ref[:, i * cols : (i + 1) * cols] = h1_ref[head * per_half + i].astype(F32)[2:3]
    router_all[...] = router_ref[...].astype(F32)
    gain = gain_ref[...].astype(F32).reshape(1, -1)
    h = jnp.concatenate([h1_ref[u].astype(F32)[:2] for u in range(units)], axis=1)
    rstd = lax.rsqrt(jnp.mean(h * h, axis=1, keepdims=True) + 1e-05)
    xn = (h * rstd * gain).astype(BF16).astype(F32)
    other = []
    for r in routed_rows(routes_ref):
        other.append(jnp.where(routes_ref[0, r] == 0, routes_ref[1, r], routes_ref[0, r]))
    first = jnp.sum(xn * router_all[0:1, :], axis=1, keepdims=True)
    second = jnp.sum(
        xn * jnp.concatenate([router_all[pl.ds(e, 1), :] for e in other], axis=0), axis=1, keepdims=True
    )
    route = 1.0 / (1.0 + jnp.exp(second - first))
    lane_ids = lax.broadcasted_iota(jnp.int32, stat_ref.shape, 1)
    stat_ref[...] = jnp.where(lane_ids == 0, rstd, route)


def down_kernel(mine_ref, other_ref, stat_ref, slot_ref, wd_ref, o_ref, full_ref):
    hidden = wd_ref.shape[0]
    rstd = stat_ref[:, 0:1]
    route = stat_ref[:, 1:2]
    gate = (mine_ref[:, :hidden] + other_ref[:, :hidden]) * rstd
    up = (mine_ref[:, hidden:] + other_ref[:, hidden:]) * (rstd * route)
    act = (gate / (1.0 + jnp.exp(-gate)) * up).astype(BF16)
    full = jnp.dot(act, wd_ref[...], preferred_element_type=F32)
    for j in range(o_ref.shape[1]):
        for s in range(2):
            full_ref[s, j : j + 1, :] = full[s : s + 1, j * LANES : (j + 1) * LANES]
    for r in range(o_ref.shape[0]):
        block = jnp.where(slot_ref[r : r + 1, 1:2] > 0.0, full_ref[1], 0.0)
        o_ref[r] = jnp.where(slot_ref[r : r + 1, 0:1] > 0.0, full_ref[0], block).astype(BF16)


def sum_kernel(parts_ref, own_ref, o_ref):
    moe = parts_ref[0].astype(F32)
    for u in range(1, parts_ref.shape[0]):
        moe = moe + parts_ref[u].astype(F32)
    for j in range(parts_ref.shape[1]):
        lanes = slice(j * LANES, (j + 1) * LANES)
        o_ref[:, lanes] = (own_ref[:, lanes] + moe[j : j + 1, :]).astype(o_ref.dtype)


SMEM = pl.BlockSpec(memory_space=pltpu.SMEM)
VMEM = pl.BlockSpec(memory_space=pltpu.VMEM)
ANY = pl.BlockSpec(memory_space=pltpu.HBM)


def in_hbm(x):
    return pltpu.with_memory_space_constraint(x, pltpu.HBM)


def in_vmem(x):
    return pltpu.with_memory_space_constraint(x, pltpu.VMEM)


def small_body(
    queries,
    fresh_key,
    fresh_value,
    key_cache_pages,
    value_cache_pages,
    page_table,
    lengths,
    resid,
    w_out,
    norm_gain,
    router,
    routes,
    w_gate,
    w_up,
    w_down,
):
    rows = routes.shape[0]
    half = w_gate.shape[0]
    chunks = half // LANES
    hidden = w_gate.shape[1]
    cols = w_out.shape[1]
    swap = [(0, 1), (1, 0)]
    routes_t = routes.T

    def exchange(x):
        return lax.all_to_all(x, "units", split_axis=0, concat_axis=0, tiled=True)

    def call(kernel, out, specs, name, scratch=(), limit=6, more=()):
        more = [in_hbm(w) for w in more]

        def whole(*refs):
            n = len(specs)
            kernel(*refs[:n], *refs[n + len(more):])

        f = pl.pallas_call(
            whole,
            out_shape=out,
            in_specs=specs + [ANY] * len(more),
            out_specs=jax.tree.map(lambda _: VMEM, out),
            scratch_shapes=scratch,
            compiler_params=pltpu.CompilerParams(vmem_limit_bytes=limit * MIB),
            name=name,
        )
        return lambda *ops: f(*ops, *more)

    begun = call(
        begin_kernel, jax.ShapeDtypeStruct((8, LANES), F32), [], "begin", more=(w_gate,)
    )()
    attn = call(
        attn_kernel,
        jax.ShapeDtypeStruct((rows, chunks, LANES), BF16),
        [VMEM, SMEM] + [VMEM] * 6,
        "attend",
        more=(w_gate, w_up, w_down),
    )(
        begun, lengths, *map(in_vmem, (page_table, queries, fresh_key, fresh_value, key_cache_pages, value_cache_pages)),
    )
    attn_all = exchange(attn)
    proj, slots = call(
        proj_kernel,
        (jax.ShapeDtypeStruct((rows, cols), F32), jax.ShapeDtypeStruct((rows, LANES), F32)),
        [VMEM] * 3,
        "proj",
    )(attn_all, in_vmem(w_out), routes_t)
    proj_other = lax.ppermute(proj, "heads", swap)
    h1_cols = call(resid_kernel, jax.ShapeDtypeStruct((rows, 4, cols), BF16), [VMEM] * 4, "resid")(
        resid, proj, proj_other, slots
    )
    h1 = exchange(h1_cols)
    gu = call(expert_kernel, jax.ShapeDtypeStruct((2, 2 * hidden), F32), [VMEM] * 4, "expert")(
        h1, norm_gain, in_vmem(w_gate), in_vmem(w_up)
    )
    gu_other = lax.ppermute(gu, "heads", swap)
    stat, own_h1 = call(
        side_kernel,
        (jax.ShapeDtypeStruct((2, LANES), F32), jax.ShapeDtypeStruct((1, half), F32)),
        [SMEM] + [VMEM] * 3,
        "side",
        scratch=(pltpu.VMEM(router.shape[::-1], F32),),
    )(routes_t, h1, norm_gain, router.T)
    full = call(
        down_kernel,
        jax.ShapeDtypeStruct((rows, chunks, LANES), BF16),
        [VMEM] * 5,
        "down",
        scratch=(pltpu.VMEM((2, chunks, LANES), F32),),
    )(gu, gu_other, stat, slots, in_vmem(w_down))
    parts = exchange(full)
    return call(sum_kernel, jax.ShapeDtypeStruct((1, half), BF16), [VMEM] * 2, "total")(
        parts, own_h1
    )


def one_tile(*args):
    queries, routes, router = args[0], args[11], args[10]
    rows = routes.shape[0]
    units = lax.axis_size("units")
    return (
        queries.shape[0] == 1
        and rows == 8
        and units == rows
        and rows * routes.shape[1] // router.shape[1] == 2
    )


def dispatch(*args):
    return small_body(*args) if one_tile(*args) else body(*args)


def solution(mesh):
    in_specs = (
        P(("groups", "units"), "heads"),
        P(("groups", "units"), "heads"),
        P(("groups", "units"), "heads"),
        P(("groups", "units"), None, "heads"),
        P(("groups", "units"), None, "heads"),
        P(("groups", "units"), None),
        P(("groups", "units")),
        P("groups", "units"),
        P("heads", "units"),
        P(),
        P(),
        P("groups", None),
        P("heads", "units"),
        P("heads", "units"),
        P("units", "heads"),
    )
    out_specs = P(("groups", "units"), "heads")
    return jax.shard_map(dispatch, mesh=mesh, in_specs=in_specs, out_specs=out_specs, check_vma=False)
```

```python
import functools

import jax
import jax.numpy as jnp
from jax import lax
from jax.experimental import pallas as pl
from jax.experimental.pallas import tpu as pltpu
from jax.sharding import PartitionSpec as P

HEAD_WIDTH = 128
LANES = 128
F32 = jnp.float32
BF16 = jnp.bfloat16
MIB = 2**20


def attend(
    queries, fresh_key, fresh_value, key_cache_pages, value_cache_pages, page_table, lengths
):
    token_rows = queries.shape[0]
    kv_width = fresh_key.shape[1]
    heads_kv = kv_width // HEAD_WIDTH
    query_group = queries.shape[1] // kv_width
    score_scale = HEAD_WIDTH ** (-0.5)
    key_rows = key_cache_pages[page_table].reshape(token_rows, -1, heads_kv, HEAD_WIDTH)
    value_rows = value_cache_pages[page_table].reshape(token_rows, -1, heads_kv, HEAD_WIDTH)
    query_grid = queries.reshape(token_rows, heads_kv, query_group, HEAD_WIDTH)
    scores = (
        jnp.einsum("rgjd,rtgd->rgjt", query_grid, key_rows, preferred_element_type=jnp.float32)
        * score_scale
    )
    expert_owned = (
        jnp.einsum(
            "fiam,fim->fia",
            query_grid,
            fresh_key.reshape(token_rows, heads_kv, HEAD_WIDTH),
            preferred_element_type=jnp.float32,
        )
        * score_scale
    )
    span = key_rows.shape[1]
    live = (jnp.arange(span, dtype=jnp.int32)[None, :] < lengths[:, None])[:, None, None, :]
    top = jnp.maximum(jnp.max(jnp.where(live, scores, -jnp.inf), axis=-1), expert_owned)
    prob = jnp.where(live, jnp.exp(scores - top[..., None]), 0.0)
    own_p = jnp.exp(expert_owned - top)
    total = jnp.sum(prob, axis=-1) + own_p
    weights = (prob / total[..., None]).astype(jnp.bfloat16)
    owned_weight = (own_p / total).astype(jnp.bfloat16)
    blended_values = jnp.einsum(
        "rgjt,rtgd->rgjd", weights, value_rows, preferred_element_type=jnp.float32
    )
    blended_values = blended_values + owned_weight.astype(jnp.float32)[
        ..., None
    ] * fresh_value.reshape(token_rows, heads_kv, 1, HEAD_WIDTH).astype(jnp.float32)
    return blended_values.reshape(token_rows, -1).astype(jnp.bfloat16)


def route_weight(logits, routes):
    picks = (
        routes[:, :, None] == jnp.arange(logits.shape[1], dtype=jnp.int32)[None, None, :]
    ).astype(jnp.float32)
    chosen = jnp.sum(picks * logits[:, None, :], axis=-1)
    first = jax.nn.sigmoid(chosen[:, 0] - chosen[:, 1])
    second = jax.nn.sigmoid(chosen[:, 1] - chosen[:, 0])
    return jnp.where(routes[:, 0] == 0, first, jnp.where(routes[:, 1] == 0, second, 0.0))


def body(
    queries,
    fresh_key,
    fresh_value,
    key_cache_pages,
    value_cache_pages,
    page_table,
    lengths,
    resid,
    w_out,
    norm_gain,
    router,
    routes,
    w_gate,
    w_up,
    w_down,
):
    own_rows = queries.shape[0]
    half_width = w_gate.shape[0]
    all_rows = routes.shape[0]
    routed_count = all_rows * routes.shape[1] // router.shape[1]
    unit_index = lax.axis_index("units")
    head_index = lax.axis_index("heads")
    attn = attend(
        queries, fresh_key, fresh_value, key_cache_pages, value_cache_pages, page_table, lengths
    )
    proj_part = jnp.dot(
        lax.all_gather(attn, "units", axis=0, tiled=True), w_out, preferred_element_type=jnp.float32
    )
    proj = lax.psum(proj_part, "heads")
    h1_cols = (resid.astype(jnp.float32) + proj).astype(jnp.bfloat16)
    h1 = lax.all_gather(h1_cols, "units", axis=1, tiled=True)
    is_routed = jnp.any(routes == 0, axis=1)
    slot_of = jnp.cumsum(is_routed.astype(jnp.int32)) - 1
    slot_ids = jnp.arange(routed_count, dtype=jnp.int32)
    row_ids = jnp.arange(all_rows, dtype=jnp.int32)
    match = (slot_of[None, :] == slot_ids[:, None]) & is_routed[None, :]
    picked_rows = jnp.sum(jnp.where(match, row_ids[None, :], 0), axis=1)
    h1_sel = h1[picked_rows]
    hf_sel = h1_sel.astype(jnp.float32)
    rstd = lax.rsqrt(jnp.mean(hf_sel * hf_sel, axis=-1, keepdims=True) + 1e-05)
    xn_sel = (hf_sel * rstd * norm_gain.astype(jnp.float32)).astype(jnp.bfloat16)
    logits = jnp.dot(xn_sel, router, preferred_element_type=jnp.float32)
    route = route_weight(logits, routes[picked_rows])
    xn_half = lax.dynamic_slice_in_dim(xn_sel, head_index * half_width, half_width, 1)
    gate_part = jnp.dot(xn_half, w_gate, preferred_element_type=jnp.float32)
    up_part = jnp.dot(xn_half, w_up, preferred_element_type=jnp.float32)
    gate, up = lax.psum((gate_part, up_part), "heads")
    hidden = (jax.nn.silu(gate) * up * route[:, None]).astype(jnp.bfloat16)
    full_term = jnp.dot(hidden, w_down, preferred_element_type=jnp.float32)
    own_start = unit_index * own_rows
    own_h1 = lax.dynamic_slice_in_dim(
        lax.dynamic_slice_in_dim(h1, own_start, own_rows, 0), head_index * half_width, half_width, 1
    )
    own_routed = lax.dynamic_slice_in_dim(is_routed, own_start, own_rows, 0)
    own_slot = jnp.maximum(lax.dynamic_slice_in_dim(slot_of, own_start, own_rows, 0), 0)
    moe_sel = lax.psum(full_term, "units")
    moe_own = jnp.where(own_routed[:, None], moe_sel[own_slot], 0.0)
    return (own_h1.astype(jnp.float32) + moe_own).astype(jnp.bfloat16)


def begin_kernel(o_ref):
    o_ref[...] = jnp.zeros(o_ref.shape, F32)


def attn_kernel(begun_ref, len_ref, table_ref, q_ref, fk_ref, fv_ref, k_ref, v_ref, o_ref):
    pages, page_tokens, kv_width = k_ref.shape
    heads_kv = kv_width // HEAD_WIDTH
    group = q_ref.shape[1] // kv_width
    rows = -(-group // 8) * 8
    scale = HEAD_WIDTH ** (-0.5)
    length = len_ref[0]
    pad = [jnp.zeros((rows - group, HEAD_WIDTH), F32)] if rows > group else []
    table = table_ref[...]
    slots = lax.broadcasted_iota(jnp.int32, table.shape, 1)
    tokens = lax.broadcasted_iota(jnp.int32, (rows, page_tokens), 1)
    live = jnp.concatenate(
        [
            tokens + page_tokens * jnp.sum(jnp.where(table == page, slots, 0), axis=1, keepdims=True) < length
            for page in range(pages)
        ],
        axis=1,
    )
    heads = [slice(g * HEAD_WIDTH, (g + 1) * HEAD_WIDTH) for g in range(heads_kv)]
    q = q_ref[...].astype(F32)
    fk = fk_ref[...].astype(F32)
    q_grid = [
        jnp.concatenate(
            [q[:, (g * group + j) * HEAD_WIDTH : (g * group + j + 1) * HEAD_WIDTH] for j in range(group)] + pad,
            axis=0,
        )
        for g in range(heads_kv)
    ]
    owns = [
        jnp.sum(q_g * fk[:, lanes], axis=1, keepdims=True) * scale for q_g, lanes in zip(q_grid, heads)
    ]
    q_grid = [q_g.astype(BF16) for q_g in q_grid]
    scores = [
        lax.dot_general(
            q_g,
            jnp.concatenate([k_ref[page, :, lanes] for page in range(pages)], axis=0),
            (((1,), (1,)), ((), ())),
            preferred_element_type=F32,
        )
        * scale
        for q_g, lanes in zip(q_grid, heads)
    ]
    weights, own_weights = [], []
    for s, own in zip(scores, owns):
        top = jnp.maximum(jnp.max(jnp.where(live, s, -jnp.inf), axis=1, keepdims=True), own)
        prob = jnp.where(live, jnp.exp(s - top), 0.0)
        own_p = jnp.exp(own - top)
        total = jnp.sum(prob, axis=1, keepdims=True) + own_p
        weights.append((prob / total).astype(BF16))
        own_weights.append((own_p / total).astype(BF16).astype(F32))
    fv = fv_ref[...].astype(F32)
    blended = [
        (
            jnp.dot(
                w,
                jnp.concatenate([v_ref[page, :, lanes] for page in range(pages)], axis=0),
                preferred_element_type=F32,
            )
            + own_w * fv[:, lanes]
        )[:group]
        for w, own_w, lanes in zip(weights, own_weights, heads)
    ]
    attn = jnp.concatenate(blended, axis=0).astype(BF16)
    for r in range(o_ref.shape[0]):
        o_ref[r] = attn


def proj_kernel(attn_ref, w_ref, routes_ref, o_ref, slot_ref):
    attn = attn_ref[...].astype(F32)
    x = jnp.concatenate([attn[:, j, :] for j in range(attn.shape[1])], axis=1).astype(BF16)
    o_ref[...] = jnp.dot(x, w_ref[...], preferred_element_type=F32)
    hit = jnp.logical_or(routes_ref[0:1, :] == 0, routes_ref[1:2, :] == 0)
    ids = lax.broadcasted_iota(jnp.int32, hit.shape, 1)
    first = jnp.min(jnp.where(hit, ids, hit.shape[1]), axis=1, keepdims=True)
    last = jnp.max(jnp.where(hit, ids, -1), axis=1, keepdims=True)
    request = lax.broadcasted_iota(jnp.int32, slot_ref.shape, 0)
    lane = lax.broadcasted_iota(jnp.int32, slot_ref.shape, 1)
    marks = jnp.where(request == jnp.where(lane == 0, first, last), 1, 0)
    named = jnp.where(routes_ref[0:1, :] == 0, routes_ref[1:2, :], routes_ref[0:1, :])
    other = [jnp.sum(jnp.where(ids == r, named, 0), axis=1, keepdims=True) for r in (first, last)]
    marks = jnp.where(lane == 2, other[0], jnp.where(lane == 3, other[1], marks))
    slot_ref[...] = marks


def resid_kernel(resid_ref, mine_ref, other_ref, slot_ref, o_ref):
    h1 = (resid_ref[...].astype(F32) + (mine_ref[...] + other_ref[...])).astype(BF16).astype(F32)
    routed = [
        jnp.sum(jnp.where(slot_ref[:, s : s + 1] > 0, h1, 0.0), axis=0, keepdims=True) for s in range(2)
    ]
    for r in range(o_ref.shape[0]):
        own = h1[r : r + 1]
        o_ref[r] = jnp.concatenate(routed + [own, own], axis=0).astype(BF16)


def first_kernel(h1_ref, gain_ref, wg_ref, wu_ref, _, gu_ref, x_ref):
    units, _, cols = h1_ref.shape
    part = wg_ref.shape[1] // 2
    per_half = units // 2
    head = lax.axis_index("heads")
    half = per_half * cols
    gain = gain_ref[...].astype(F32).reshape(1, -1)
    gain = jnp.where(head == 0, gain[:, :half], gain[:, half:])
    h1 = jnp.concatenate([h1_ref[head * per_half + i].astype(F32)[:2] for i in range(per_half)], axis=1)
    x = (h1 * gain).astype(BF16)
    x_ref[...] = x
    gu_ref[:, :part] = jnp.dot(x, wg_ref[:, :part], preferred_element_type=F32)
    gu_ref[:, part:] = jnp.dot(x, wu_ref[:, :part], preferred_element_type=F32)


def second_kernel(
    x_ref, wg_ref, wu_ref, h1_ref, gain_ref, router_ref, slot_ref, _, gu_ref, stat_ref, own_ref
):
    part = wg_ref.shape[1] // 2
    x = x_ref[...]
    gu_ref[:, :part] = jnp.dot(x, wg_ref[:, part:], preferred_element_type=F32)
    gu_ref[:, part:] = jnp.dot(x, wu_ref[:, part:], preferred_element_type=F32)
    units, _, cols = h1_ref.shape
    per_half = units // 2
    head = lax.axis_index("heads")
    for i in range(per_half):
        own_ref[:, i * cols : (i + 1) * cols] = h1_ref[head * per_half + i].astype(F32)[2:3]
    gain = gain_ref[...].astype(F32).reshape(1, -1)
    router = router_ref[...].astype(F32)
    expert = lax.broadcasted_iota(jnp.int32, (router.shape[0], 1), 0)
    h = jnp.concatenate([h1_ref[u].astype(F32)[:2] for u in range(units)], axis=1)
    rstd = lax.rsqrt(jnp.mean(h * h, axis=1, keepdims=True) + 1e-05)
    xn = (h * rstd * gain).astype(BF16).astype(F32)
    lane_ids = lax.broadcasted_iota(jnp.int32, (1, LANES), 1)
    for s in range(2):
        logits = jnp.sum(router * xn[s : s + 1], axis=1, keepdims=True)
        other = slot_ref[0:1, 2 + s : 3 + s]
        diff = jnp.sum(
            jnp.where(expert == other, logits, 0.0) - jnp.where(expert == 0, logits, 0.0),
            axis=0,
            keepdims=True,
        )
        route = 1.0 / (1.0 + jnp.exp(diff))
        stat_ref[s : s + 1, :] = jnp.where(lane_ids == 0, rstd[s : s + 1], route)


def activate(mine_ref, other_ref, stat_ref):
    part = mine_ref.shape[1] // 2
    rstd = stat_ref[:, 0:1]
    route = stat_ref[:, 1:2]
    gate = (mine_ref[:, :part] + other_ref[:, :part]) * rstd
    up = (mine_ref[:, part:] + other_ref[:, part:]) * (rstd * route)
    return (gate / (1.0 + jnp.exp(-gate)) * up).astype(BF16)


def down_first_kernel(mine_ref, other_ref, stat_ref, wd_ref, o_ref):
    act = activate(mine_ref, other_ref, stat_ref)
    o_ref[...] = jnp.dot(act, wd_ref[: act.shape[1], :], preferred_element_type=F32)


def down_second_kernel(mine_ref, other_ref, stat_ref, wd_ref, before_ref, slot_ref, o_ref, full_ref):
    act = activate(mine_ref, other_ref, stat_ref)
    full = before_ref[...] + jnp.dot(act, wd_ref[act.shape[1] :, :], preferred_element_type=F32)
    for j in range(o_ref.shape[1]):
        for s in range(2):
            full_ref[s, j : j + 1, :] = full[s : s + 1, j * LANES : (j + 1) * LANES]
    for r in range(o_ref.shape[0]):
        block = jnp.where(slot_ref[r : r + 1, 1:2] > 0, full_ref[1], 0.0)
        o_ref[r] = jnp.where(slot_ref[r : r + 1, 0:1] > 0, full_ref[0], block).astype(BF16)


def sum_kernel(parts_ref, own_ref, o_ref):
    moe = parts_ref[0].astype(F32)
    for u in range(1, parts_ref.shape[0]):
        moe = moe + parts_ref[u].astype(F32)
    for j in range(parts_ref.shape[1]):
        lanes = slice(j * LANES, (j + 1) * LANES)
        o_ref[:, lanes] = (own_ref[:, lanes] + moe[j : j + 1, :]).astype(o_ref.dtype)


SMEM = pl.BlockSpec(memory_space=pltpu.SMEM)
VMEM = pl.BlockSpec(memory_space=pltpu.VMEM)
ANY = pl.BlockSpec(memory_space=pltpu.HBM)


def in_hbm(x):
    return pltpu.with_memory_space_constraint(x, pltpu.HBM)


def in_vmem(x):
    return pltpu.with_memory_space_constraint(x, pltpu.VMEM)


def small_body(
    queries,
    fresh_key,
    fresh_value,
    key_cache_pages,
    value_cache_pages,
    page_table,
    lengths,
    resid,
    w_out,
    norm_gain,
    router,
    routes,
    w_gate,
    w_up,
    w_down,
):
    rows = routes.shape[0]
    half = w_gate.shape[0]
    chunks = half // LANES
    hidden = w_gate.shape[1]
    cols = w_out.shape[1]
    swap = [(0, 1), (1, 0)]
    routes_t = routes.T

    def exchange(x):
        return lax.all_to_all(x, "units", split_axis=0, concat_axis=0, tiled=True)

    def call(kernel, out, specs, name, scratch=(), limit=6, more=()):
        more = [in_hbm(w) for w in more]

        def whole(*refs):
            n = len(specs)
            kernel(*refs[:n], *refs[n + len(more):])

        f = pl.pallas_call(
            whole,
            out_shape=out,
            in_specs=specs + [ANY] * len(more),
            out_specs=jax.tree.map(lambda _: VMEM, out),
            scratch_shapes=scratch,
            compiler_params=pltpu.CompilerParams(vmem_limit_bytes=limit * MIB),
            name=name,
        )
        return lambda *ops: f(*ops, *more)

    begun = call(
        begin_kernel, jax.ShapeDtypeStruct((8, LANES), F32), [], "begin", more=(w_gate,)
    )()
    attn = call(
        attn_kernel,
        jax.ShapeDtypeStruct((rows, chunks, LANES), BF16),
        [VMEM, SMEM] + [VMEM] * 6,
        "attend",
        more=(w_gate, w_up, w_down),
    )(
        begun, lengths, *map(in_vmem, (page_table, queries, fresh_key, fresh_value, key_cache_pages, value_cache_pages)),
    )
    attn_all = exchange(attn)
    proj, slots = call(
        proj_kernel,
        (jax.ShapeDtypeStruct((rows, cols), F32), jax.ShapeDtypeStruct((rows, LANES), jnp.int32)),
        [VMEM] * 3,
        "proj",
    )(attn_all, in_vmem(w_out), routes_t)
    proj_other = lax.ppermute(proj, "heads", swap)
    h1_cols = call(resid_kernel, jax.ShapeDtypeStruct((rows, 4, cols), BF16), [VMEM] * 4, "resid")(
        resid, proj, proj_other, slots
    )
    h1 = exchange(h1_cols)
    weights = (in_vmem(w_gate), in_vmem(w_up))
    w_down_near = in_vmem(w_down)
    gu, x = call(
        first_kernel,
        (jax.ShapeDtypeStruct((2, hidden), F32), jax.ShapeDtypeStruct((2, half), BF16)),
        [VMEM] * 5,
        "first",
    )(h1, norm_gain, *weights, w_down_near)
    gu_other = lax.ppermute(gu, "heads", swap)
    gu_late, stat, own_h1 = call(
        second_kernel,
        (
            jax.ShapeDtypeStruct((2, hidden), F32),
            jax.ShapeDtypeStruct((2, LANES), F32),
            jax.ShapeDtypeStruct((1, half), F32),
        ),
        [VMEM] * 8,
        "second",
    )(x, *weights, h1, norm_gain, router.T, slots, w_down_near)
    gu_late_other = lax.ppermute(gu_late, "heads", swap)
    before = call(down_first_kernel, jax.ShapeDtypeStruct((2, half), F32), [VMEM] * 4, "down_first")(
        gu, gu_other, stat, w_down_near
    )
    full = call(
        down_second_kernel,
        jax.ShapeDtypeStruct((rows, chunks, LANES), BF16),
        [VMEM] * 6,
        "down_second",
        scratch=(pltpu.VMEM((2, chunks, LANES), F32),),
    )(gu_late, gu_late_other, stat, w_down_near, before, slots)
    parts = exchange(full)
    return call(sum_kernel, jax.ShapeDtypeStruct((1, half), BF16), [VMEM] * 2, "total")(
        parts, own_h1
    )


def one_tile(*args):
    queries, routes, router = args[0], args[11], args[10]
    rows = routes.shape[0]
    units = lax.axis_size("units")
    return (
        queries.shape[0] == 1
        and rows == 8
        and units == rows
        and rows * routes.shape[1] // router.shape[1] == 2
    )


def dispatch(*args):
    return small_body(*args) if one_tile(*args) else body(*args)


def solution(mesh):
    in_specs = (
        P(("groups", "units"), "heads"),
        P(("groups", "units"), "heads"),
        P(("groups", "units"), "heads"),
        P(("groups", "units"), None, "heads"),
        P(("groups", "units"), None, "heads"),
        P(("groups", "units"), None),
        P(("groups", "units")),
        P("groups", "units"),
        P("heads", "units"),
        P(),
        P(),
        P("groups", None),
        P("heads", "units"),
        P("heads", "units"),
        P("units", "heads"),
    )
    out_specs = P(("groups", "units"), "heads")
    return jax.shard_map(dispatch, mesh=mesh, in_specs=in_specs, out_specs=out_specs, check_vma=False)
```

```python
import functools

import jax
import jax.numpy as jnp
from jax import lax
from jax.experimental import pallas as pl
from jax.experimental.pallas import tpu as pltpu
from jax.sharding import PartitionSpec as P

HEAD_WIDTH = 128
LANES = 128
F32 = jnp.float32
BF16 = jnp.bfloat16
MIB = 2**20
AHEAD_PARTS = 4


def attend(
    queries, fresh_key, fresh_value, key_cache_pages, value_cache_pages, page_table, lengths
):
    token_rows = queries.shape[0]
    kv_width = fresh_key.shape[1]
    heads_kv = kv_width // HEAD_WIDTH
    query_group = queries.shape[1] // kv_width
    score_scale = HEAD_WIDTH ** (-0.5)
    key_rows = key_cache_pages[page_table].reshape(token_rows, -1, heads_kv, HEAD_WIDTH)
    value_rows = value_cache_pages[page_table].reshape(token_rows, -1, heads_kv, HEAD_WIDTH)
    query_grid = queries.reshape(token_rows, heads_kv, query_group, HEAD_WIDTH)
    scores = (
        jnp.einsum("rgjd,rtgd->rgjt", query_grid, key_rows, preferred_element_type=jnp.float32)
        * score_scale
    )
    expert_owned = (
        jnp.einsum(
            "fiam,fim->fia",
            query_grid,
            fresh_key.reshape(token_rows, heads_kv, HEAD_WIDTH),
            preferred_element_type=jnp.float32,
        )
        * score_scale
    )
    span = key_rows.shape[1]
    live = (jnp.arange(span, dtype=jnp.int32)[None, :] < lengths[:, None])[:, None, None, :]
    top = jnp.maximum(jnp.max(jnp.where(live, scores, -jnp.inf), axis=-1), expert_owned)
    prob = jnp.where(live, jnp.exp(scores - top[..., None]), 0.0)
    own_p = jnp.exp(expert_owned - top)
    total = jnp.sum(prob, axis=-1) + own_p
    weights = (prob / total[..., None]).astype(jnp.bfloat16)
    owned_weight = (own_p / total).astype(jnp.bfloat16)
    blended_values = jnp.einsum(
        "rgjt,rtgd->rgjd", weights, value_rows, preferred_element_type=jnp.float32
    )
    blended_values = blended_values + owned_weight.astype(jnp.float32)[
        ..., None
    ] * fresh_value.reshape(token_rows, heads_kv, 1, HEAD_WIDTH).astype(jnp.float32)
    return blended_values.reshape(token_rows, -1).astype(jnp.bfloat16)


def route_weight(logits, routes):
    picks = (
        routes[:, :, None] == jnp.arange(logits.shape[1], dtype=jnp.int32)[None, None, :]
    ).astype(jnp.float32)
    chosen = jnp.sum(picks * logits[:, None, :], axis=-1)
    first = jax.nn.sigmoid(chosen[:, 0] - chosen[:, 1])
    second = jax.nn.sigmoid(chosen[:, 1] - chosen[:, 0])
    return jnp.where(routes[:, 0] == 0, first, jnp.where(routes[:, 1] == 0, second, 0.0))


def body(
    queries,
    fresh_key,
    fresh_value,
    key_cache_pages,
    value_cache_pages,
    page_table,
    lengths,
    resid,
    w_out,
    norm_gain,
    router,
    routes,
    w_gate,
    w_up,
    w_down,
):
    own_rows = queries.shape[0]
    half_width = w_gate.shape[0]
    all_rows = routes.shape[0]
    routed_count = all_rows * routes.shape[1] // router.shape[1]
    unit_index = lax.axis_index("units")
    head_index = lax.axis_index("heads")
    attn = attend(
        queries, fresh_key, fresh_value, key_cache_pages, value_cache_pages, page_table, lengths
    )
    proj_part = jnp.dot(
        lax.all_gather(attn, "units", axis=0, tiled=True), w_out, preferred_element_type=jnp.float32
    )
    proj = lax.psum(proj_part, "heads")
    h1_cols = (resid.astype(jnp.float32) + proj).astype(jnp.bfloat16)
    h1 = lax.all_gather(h1_cols, "units", axis=1, tiled=True)
    is_routed = jnp.any(routes == 0, axis=1)
    slot_of = jnp.cumsum(is_routed.astype(jnp.int32)) - 1
    slot_ids = jnp.arange(routed_count, dtype=jnp.int32)
    row_ids = jnp.arange(all_rows, dtype=jnp.int32)
    match = (slot_of[None, :] == slot_ids[:, None]) & is_routed[None, :]
    picked_rows = jnp.sum(jnp.where(match, row_ids[None, :], 0), axis=1)
    h1_sel = h1[picked_rows]
    hf_sel = h1_sel.astype(jnp.float32)
    rstd = lax.rsqrt(jnp.mean(hf_sel * hf_sel, axis=-1, keepdims=True) + 1e-05)
    xn_sel = (hf_sel * rstd * norm_gain.astype(jnp.float32)).astype(jnp.bfloat16)
    logits = jnp.dot(xn_sel, router, preferred_element_type=jnp.float32)
    route = route_weight(logits, routes[picked_rows])
    xn_half = lax.dynamic_slice_in_dim(xn_sel, head_index * half_width, half_width, 1)
    gate_part = jnp.dot(xn_half, w_gate, preferred_element_type=jnp.float32)
    up_part = jnp.dot(xn_half, w_up, preferred_element_type=jnp.float32)
    gate, up = lax.psum((gate_part, up_part), "heads")
    hidden = (jax.nn.silu(gate) * up * route[:, None]).astype(jnp.bfloat16)
    full_term = jnp.dot(hidden, w_down, preferred_element_type=jnp.float32)
    own_start = unit_index * own_rows
    own_h1 = lax.dynamic_slice_in_dim(
        lax.dynamic_slice_in_dim(h1, own_start, own_rows, 0), head_index * half_width, half_width, 1
    )
    own_routed = lax.dynamic_slice_in_dim(is_routed, own_start, own_rows, 0)
    own_slot = jnp.maximum(lax.dynamic_slice_in_dim(slot_of, own_start, own_rows, 0), 0)
    moe_sel = lax.psum(full_term, "units")
    moe_own = jnp.where(own_routed[:, None], moe_sel[own_slot], 0.0)
    return (own_h1.astype(jnp.float32) + moe_own).astype(jnp.bfloat16)


def begin_kernel(o_ref):
    o_ref[...] = jnp.zeros(o_ref.shape, F32)


def attn_kernel(begun_ref, len_ref, table_ref, q_ref, fk_ref, fv_ref, k_ref, v_ref, o_ref):
    pages, page_tokens, kv_width = k_ref.shape
    heads_kv = kv_width // HEAD_WIDTH
    group = q_ref.shape[1] // kv_width
    rows = -(-group // 8) * 8
    scale = HEAD_WIDTH ** (-0.5)
    length = len_ref[0]
    pad = [jnp.zeros((rows - group, HEAD_WIDTH), F32)] if rows > group else []
    table = table_ref[...]
    slots = lax.broadcasted_iota(jnp.int32, table.shape, 1)
    tokens = lax.broadcasted_iota(jnp.int32, (rows, page_tokens), 1)
    live = jnp.concatenate(
        [
            tokens + page_tokens * jnp.sum(jnp.where(table == page, slots, 0), axis=1, keepdims=True) < length
            for page in range(pages)
        ],
        axis=1,
    )
    heads = [slice(g * HEAD_WIDTH, (g + 1) * HEAD_WIDTH) for g in range(heads_kv)]
    q = q_ref[...].astype(F32)
    fk = fk_ref[...].astype(F32)
    q_grid = [
        jnp.concatenate(
            [q[:, (g * group + j) * HEAD_WIDTH : (g * group + j + 1) * HEAD_WIDTH] for j in range(group)] + pad,
            axis=0,
        )
        for g in range(heads_kv)
    ]
    owns = [
        jnp.sum(q_g * fk[:, lanes], axis=1, keepdims=True) * scale for q_g, lanes in zip(q_grid, heads)
    ]
    q_grid = [q_g.astype(BF16) for q_g in q_grid]
    scores = [
        lax.dot_general(
            q_g,
            jnp.concatenate([k_ref[page, :, lanes] for page in range(pages)], axis=0),
            (((1,), (1,)), ((), ())),
            preferred_element_type=F32,
        )
        * scale
        for q_g, lanes in zip(q_grid, heads)
    ]
    weights, own_weights = [], []
    for s, own in zip(scores, owns):
        top = jnp.maximum(jnp.max(jnp.where(live, s, -jnp.inf), axis=1, keepdims=True), own)
        prob = jnp.where(live, jnp.exp(s - top), 0.0)
        own_p = jnp.exp(own - top)
        total = jnp.sum(prob, axis=1, keepdims=True) + own_p
        weights.append((prob / total).astype(BF16))
        own_weights.append((own_p / total).astype(BF16).astype(F32))
    fv = fv_ref[...].astype(F32)
    blended = [
        (
            jnp.dot(
                w,
                jnp.concatenate([v_ref[page, :, lanes] for page in range(pages)], axis=0),
                preferred_element_type=F32,
            )
            + own_w * fv[:, lanes]
        )[:group]
        for w, own_w, lanes in zip(weights, own_weights, heads)
    ]
    attn = jnp.concatenate(blended, axis=0).astype(BF16)
    for r in range(o_ref.shape[0]):
        o_ref[r] = attn


def proj_kernel(attn_ref, w_ref, routes_ref, o_ref, slot_ref):
    attn = attn_ref[...].astype(F32)
    x = jnp.concatenate([attn[:, j, :] for j in range(attn.shape[1])], axis=1).astype(BF16)
    o_ref[...] = jnp.dot(x, w_ref[...], preferred_element_type=F32)
    hit = jnp.logical_or(routes_ref[0:1, :] == 0, routes_ref[1:2, :] == 0)
    ids = lax.broadcasted_iota(jnp.int32, hit.shape, 1)
    first = jnp.min(jnp.where(hit, ids, hit.shape[1]), axis=1, keepdims=True)
    last = jnp.max(jnp.where(hit, ids, -1), axis=1, keepdims=True)
    request = lax.broadcasted_iota(jnp.int32, slot_ref.shape, 0)
    lane = lax.broadcasted_iota(jnp.int32, slot_ref.shape, 1)
    marks = jnp.where(request == jnp.where(lane == 0, first, last), 1, 0)
    named = jnp.where(routes_ref[0:1, :] == 0, routes_ref[1:2, :], routes_ref[0:1, :])
    other = [jnp.sum(jnp.where(ids == r, named, 0), axis=1, keepdims=True) for r in (first, last)]
    marks = jnp.where(lane == 2, other[0], jnp.where(lane == 3, other[1], marks))
    slot_ref[...] = marks


def resid_kernel(resid_ref, mine_ref, other_ref, slot_ref, o_ref):
    h1 = (resid_ref[...].astype(F32) + (mine_ref[...] + other_ref[...])).astype(BF16).astype(F32)
    routed = [
        jnp.sum(jnp.where(slot_ref[:, s : s + 1] > 0, h1, 0.0), axis=0, keepdims=True) for s in range(2)
    ]
    for r in range(o_ref.shape[0]):
        own = h1[r : r + 1]
        o_ref[r] = jnp.concatenate(routed + [own, own], axis=0).astype(BF16)


def gate_up(x, w_refs, o_ref, start, stop, at, width):
    for i, w_ref in enumerate(w_refs):
        lanes = slice(i * width + at, i * width + at + stop - start)
        o_ref[:, lanes] = jnp.dot(x, w_ref[:, start:stop], preferred_element_type=F32)


def scales(h1_ref, gain_ref, router_ref, slot_ref):
    gain = gain_ref[...].astype(F32).reshape(1, -1)
    router = router_ref[...].astype(F32)
    expert = lax.broadcasted_iota(jnp.int32, (router.shape[0], 1), 0)
    h = jnp.concatenate([h1_ref[u].astype(F32)[:2] for u in range(h1_ref.shape[0])], axis=1)
    rstd = lax.rsqrt(jnp.mean(h * h, axis=1, keepdims=True) + 1e-05)
    xn = (h * rstd * gain).astype(BF16).astype(F32)
    lane_ids = lax.broadcasted_iota(jnp.int32, (1, LANES), 1)
    rows = []
    for s in range(2):
        logits = jnp.sum(router * xn[s : s + 1], axis=1, keepdims=True)
        other = slot_ref[0:1, 2 + s : 3 + s]
        diff = jnp.sum(
            jnp.where(expert == other, logits, 0.0) - jnp.where(expert == 0, logits, 0.0),
            axis=0,
            keepdims=True,
        )
        route = 1.0 / (1.0 + jnp.exp(diff))
        rows.append(jnp.where(lane_ids == 0, rstd[s : s + 1], route))
    return jnp.concatenate(rows, axis=0)


def first_kernel(
    h1_ref, gain_ref, wg_ref, wu_ref, router_ref, slot_ref, _, gu_ref, x_ref, ahead_ref
):
    units, _, cols = h1_ref.shape
    part = wg_ref.shape[1] // 2
    ahead = ahead_ref.shape[1] // 2
    per_half = units // 2
    head = lax.axis_index("heads")
    half = per_half * cols
    gain = gain_ref[...].astype(F32).reshape(1, -1)
    gain = jnp.where(head == 0, gain[:, :half], gain[:, half:])
    h1 = jnp.concatenate([h1_ref[head * per_half + i].astype(F32)[:2] for i in range(per_half)], axis=1)
    x = (h1 * gain).astype(BF16)
    x_ref[...] = x
    gate_up(x, (wg_ref, wu_ref), gu_ref, 0, part, 0, part)

    @pl.when(head == 1)
    def _():
        gate_up(x_ref[...], (wg_ref, wu_ref), ahead_ref, part, part + ahead, 0, ahead)
        gu_ref[:, 2 * part :] = scales(h1_ref, gain_ref, router_ref, slot_ref)

    @pl.when(head == 0)
    def _():
        ahead_ref[...] = jnp.zeros(ahead_ref.shape, F32)
        gu_ref[:, 2 * part :] = jnp.zeros((gu_ref.shape[0], LANES), F32)


def second_kernel(
    x_ref, wg_ref, wu_ref, h1_ref, ahead_ref, _, gu_ref, own_ref
):
    part = wg_ref.shape[1] // 2
    ahead = ahead_ref.shape[1] // 2
    first_core = lax.axis_index("heads") == 0

    @pl.when(first_core)
    def _():
        gate_up(x_ref[...], (wg_ref, wu_ref), gu_ref, part, part + ahead, 0, part)

    @pl.when(jnp.logical_not(first_core))
    def _():
        gu_ref[:, :ahead] = ahead_ref[:, :ahead]
        gu_ref[:, part : part + ahead] = ahead_ref[:, ahead:]

    gate_up(x_ref[...], (wg_ref, wu_ref), gu_ref, part + ahead, 2 * part, ahead, part)
    units, _, cols = h1_ref.shape
    per_half = units // 2
    head = lax.axis_index("heads")
    for i in range(per_half):
        own_ref[:, i * cols : (i + 1) * cols] = h1_ref[head * per_half + i].astype(F32)[2:3]


def activate(mine_ref, other_ref, stat, part):
    rstd = stat[:, 0:1]
    route = stat[:, 1:2]
    gate = (mine_ref[:, :part] + other_ref[:, :part]) * rstd
    up = (mine_ref[:, part : 2 * part] + other_ref[:, part : 2 * part]) * (rstd * route)
    return (gate / (1.0 + jnp.exp(-gate)) * up).astype(BF16)


def down_first_kernel(mine_ref, other_ref, wd_ref, o_ref, stat_ref):
    part = wd_ref.shape[0] // 2
    stat = mine_ref[:, 2 * part :] + other_ref[:, 2 * part :]
    stat_ref[...] = stat
    act = activate(mine_ref, other_ref, stat, part)
    o_ref[...] = jnp.dot(act, wd_ref[:part, :], preferred_element_type=F32)


def down_second_kernel(mine_ref, other_ref, stat_ref, wd_ref, before_ref, slot_ref, o_ref, full_ref):
    part = wd_ref.shape[0] // 2
    act = activate(mine_ref, other_ref, stat_ref[...], part)
    full = before_ref[...] + jnp.dot(act, wd_ref[part:, :], preferred_element_type=F32)
    for j in range(o_ref.shape[1]):
        for s in range(2):
            full_ref[s, j : j + 1, :] = full[s : s + 1, j * LANES : (j + 1) * LANES]
    for r in range(o_ref.shape[0]):
        block = jnp.where(slot_ref[r : r + 1, 1:2] > 0, full_ref[1], 0.0)
        o_ref[r] = jnp.where(slot_ref[r : r + 1, 0:1] > 0, full_ref[0], block).astype(BF16)


def sum_kernel(parts_ref, own_ref, o_ref):
    moe = parts_ref[0].astype(F32)
    for u in range(1, parts_ref.shape[0]):
        moe = moe + parts_ref[u].astype(F32)
    for j in range(parts_ref.shape[1]):
        lanes = slice(j * LANES, (j + 1) * LANES)
        o_ref[:, lanes] = (own_ref[:, lanes] + moe[j : j + 1, :]).astype(o_ref.dtype)


SMEM = pl.BlockSpec(memory_space=pltpu.SMEM)
VMEM = pl.BlockSpec(memory_space=pltpu.VMEM)
ANY = pl.BlockSpec(memory_space=pltpu.HBM)


def in_hbm(x):
    return pltpu.with_memory_space_constraint(x, pltpu.HBM)


def in_vmem(x):
    return pltpu.with_memory_space_constraint(x, pltpu.VMEM)


def small_body(
    queries,
    fresh_key,
    fresh_value,
    key_cache_pages,
    value_cache_pages,
    page_table,
    lengths,
    resid,
    w_out,
    norm_gain,
    router,
    routes,
    w_gate,
    w_up,
    w_down,
):
    rows = routes.shape[0]
    half = w_gate.shape[0]
    chunks = half // LANES
    hidden = w_gate.shape[1]
    cols = w_out.shape[1]
    swap = [(0, 1), (1, 0)]
    routes_t = routes.T

    def exchange(x):
        return lax.all_to_all(x, "units", split_axis=0, concat_axis=0, tiled=True)

    def call(kernel, out, specs, name, scratch=(), limit=6, more=()):
        more = [in_hbm(w) for w in more]

        def whole(*refs):
            n = len(specs)
            kernel(*refs[:n], *refs[n + len(more):])

        f = pl.pallas_call(
            whole,
            out_shape=out,
            in_specs=specs + [ANY] * len(more),
            out_specs=jax.tree.map(lambda _: VMEM, out),
            scratch_shapes=scratch,
            compiler_params=pltpu.CompilerParams(vmem_limit_bytes=limit * MIB),
            name=name,
        )
        return lambda *ops: f(*ops, *more)

    begun = call(
        begin_kernel, jax.ShapeDtypeStruct((8, LANES), F32), [], "begin", more=(w_gate,)
    )()
    attn = call(
        attn_kernel,
        jax.ShapeDtypeStruct((rows, chunks, LANES), BF16),
        [VMEM, SMEM] + [VMEM] * 6,
        "attend",
        more=(w_gate, w_up, w_down),
    )(
        begun, lengths, *map(in_vmem, (page_table, queries, fresh_key, fresh_value, key_cache_pages, value_cache_pages)),
    )
    attn_all = exchange(attn)
    proj, slots = call(
        proj_kernel,
        (jax.ShapeDtypeStruct((rows, cols), F32), jax.ShapeDtypeStruct((rows, LANES), jnp.int32)),
        [VMEM] * 3,
        "proj",
    )(attn_all, in_vmem(w_out), routes_t)
    proj_other = lax.ppermute(proj, "heads", swap)
    h1_cols = call(resid_kernel, jax.ShapeDtypeStruct((rows, 4, cols), BF16), [VMEM] * 4, "resid")(
        resid, proj, proj_other, slots
    )
    h1 = exchange(h1_cols)
    weights = (in_vmem(w_gate), in_vmem(w_up))
    w_down_near = in_vmem(w_down)
    gu, x, ahead = call(
        first_kernel,
        (
            jax.ShapeDtypeStruct((2, hidden + LANES), F32),
            jax.ShapeDtypeStruct((2, half), BF16),
            jax.ShapeDtypeStruct((2, 2 * AHEAD_PARTS * (hidden // 16)), F32),
        ),
        [VMEM] * 7,
        "first",
    )(h1, norm_gain, *weights, router.T, slots, w_down_near)
    gu_other = lax.ppermute(gu, "heads", swap)
    gu_late, own_h1 = call(
        second_kernel,
        (jax.ShapeDtypeStruct((2, hidden), F32), jax.ShapeDtypeStruct((1, half), F32)),
        [VMEM] * 6,
        "second",
    )(x, *weights, h1, ahead, w_down_near)
    gu_late_other = lax.ppermute(gu_late, "heads", swap)
    before, stat = call(
        down_first_kernel,
        (jax.ShapeDtypeStruct((2, half), F32), jax.ShapeDtypeStruct((2, LANES), F32)),
        [VMEM] * 3,
        "down_first",
    )(gu, gu_other, w_down_near)
    full = call(
        down_second_kernel,
        jax.ShapeDtypeStruct((rows, chunks, LANES), BF16),
        [VMEM] * 6,
        "down_second",
        scratch=(pltpu.VMEM((2, chunks, LANES), F32),),
    )(gu_late, gu_late_other, stat, w_down_near, before, slots)
    parts = exchange(full)
    return call(sum_kernel, jax.ShapeDtypeStruct((1, half), BF16), [VMEM] * 2, "total")(
        parts, own_h1
    )


def one_tile(*args):
    queries, routes, router = args[0], args[11], args[10]
    rows = routes.shape[0]
    units = lax.axis_size("units")
    return (
        queries.shape[0] == 1
        and rows == 8
        and units == rows
        and rows * routes.shape[1] // router.shape[1] == 2
    )


def dispatch(*args):
    return small_body(*args) if one_tile(*args) else body(*args)


def solution(mesh):
    in_specs = (
        P(("groups", "units"), "heads"),
        P(("groups", "units"), "heads"),
        P(("groups", "units"), "heads"),
        P(("groups", "units"), None, "heads"),
        P(("groups", "units"), None, "heads"),
        P(("groups", "units"), None),
        P(("groups", "units")),
        P("groups", "units"),
        P("heads", "units"),
        P(),
        P(),
        P("groups", None),
        P("heads", "units"),
        P("heads", "units"),
        P("units", "heads"),
    )
    out_specs = P(("groups", "units"), "heads")
    return jax.shard_map(dispatch, mesh=mesh, in_specs=in_specs, out_specs=out_specs, check_vma=False)
```

```python
import functools

import jax
import jax.numpy as jnp
from jax import lax
from jax.experimental import pallas as pl
from jax.experimental.pallas import tpu as pltpu
from jax.sharding import PartitionSpec as P

HEAD_WIDTH = 128
LANES = 128
F32 = jnp.float32
BF16 = jnp.bfloat16
MIB = 2**20
AHEAD_PARTS = 2


def attend(
    queries, fresh_key, fresh_value, key_cache_pages, value_cache_pages, page_table, lengths
):
    token_rows = queries.shape[0]
    kv_width = fresh_key.shape[1]
    heads_kv = kv_width // HEAD_WIDTH
    query_group = queries.shape[1] // kv_width
    score_scale = HEAD_WIDTH ** (-0.5)
    key_rows = key_cache_pages[page_table].reshape(token_rows, -1, heads_kv, HEAD_WIDTH)
    value_rows = value_cache_pages[page_table].reshape(token_rows, -1, heads_kv, HEAD_WIDTH)
    query_grid = queries.reshape(token_rows, heads_kv, query_group, HEAD_WIDTH)
    scores = (
        jnp.einsum("rgjd,rtgd->rgjt", query_grid, key_rows, preferred_element_type=jnp.float32)
        * score_scale
    )
    expert_owned = (
        jnp.einsum(
            "fiam,fim->fia",
            query_grid,
            fresh_key.reshape(token_rows, heads_kv, HEAD_WIDTH),
            preferred_element_type=jnp.float32,
        )
        * score_scale
    )
    span = key_rows.shape[1]
    live = (jnp.arange(span, dtype=jnp.int32)[None, :] < lengths[:, None])[:, None, None, :]
    top = jnp.maximum(jnp.max(jnp.where(live, scores, -jnp.inf), axis=-1), expert_owned)
    prob = jnp.where(live, jnp.exp(scores - top[..., None]), 0.0)
    own_p = jnp.exp(expert_owned - top)
    total = jnp.sum(prob, axis=-1) + own_p
    weights = (prob / total[..., None]).astype(jnp.bfloat16)
    owned_weight = (own_p / total).astype(jnp.bfloat16)
    blended_values = jnp.einsum(
        "rgjt,rtgd->rgjd", weights, value_rows, preferred_element_type=jnp.float32
    )
    blended_values = blended_values + owned_weight.astype(jnp.float32)[
        ..., None
    ] * fresh_value.reshape(token_rows, heads_kv, 1, HEAD_WIDTH).astype(jnp.float32)
    return blended_values.reshape(token_rows, -1).astype(jnp.bfloat16)


def route_weight(logits, routes):
    picks = (
        routes[:, :, None] == jnp.arange(logits.shape[1], dtype=jnp.int32)[None, None, :]
    ).astype(jnp.float32)
    chosen = jnp.sum(picks * logits[:, None, :], axis=-1)
    first = jax.nn.sigmoid(chosen[:, 0] - chosen[:, 1])
    second = jax.nn.sigmoid(chosen[:, 1] - chosen[:, 0])
    return jnp.where(routes[:, 0] == 0, first, jnp.where(routes[:, 1] == 0, second, 0.0))


def body(
    queries,
    fresh_key,
    fresh_value,
    key_cache_pages,
    value_cache_pages,
    page_table,
    lengths,
    resid,
    w_out,
    norm_gain,
    router,
    routes,
    w_gate,
    w_up,
    w_down,
):
    own_rows = queries.shape[0]
    half_width = w_gate.shape[0]
    all_rows = routes.shape[0]
    routed_count = all_rows * routes.shape[1] // router.shape[1]
    unit_index = lax.axis_index("units")
    head_index = lax.axis_index("heads")
    attn = attend(
        queries, fresh_key, fresh_value, key_cache_pages, value_cache_pages, page_table, lengths
    )
    proj_part = jnp.dot(
        lax.all_gather(attn, "units", axis=0, tiled=True), w_out, preferred_element_type=jnp.float32
    )
    proj = lax.psum(proj_part, "heads")
    h1_cols = (resid.astype(jnp.float32) + proj).astype(jnp.bfloat16)
    h1 = lax.all_gather(h1_cols, "units", axis=1, tiled=True)
    is_routed = jnp.any(routes == 0, axis=1)
    slot_of = jnp.cumsum(is_routed.astype(jnp.int32)) - 1
    slot_ids = jnp.arange(routed_count, dtype=jnp.int32)
    row_ids = jnp.arange(all_rows, dtype=jnp.int32)
    match = (slot_of[None, :] == slot_ids[:, None]) & is_routed[None, :]
    picked_rows = jnp.sum(jnp.where(match, row_ids[None, :], 0), axis=1)
    h1_sel = h1[picked_rows]
    hf_sel = h1_sel.astype(jnp.float32)
    rstd = lax.rsqrt(jnp.mean(hf_sel * hf_sel, axis=-1, keepdims=True) + 1e-05)
    xn_sel = (hf_sel * rstd * norm_gain.astype(jnp.float32)).astype(jnp.bfloat16)
    logits = jnp.dot(xn_sel, router, preferred_element_type=jnp.float32)
    route = route_weight(logits, routes[picked_rows])
    xn_half = lax.dynamic_slice_in_dim(xn_sel, head_index * half_width, half_width, 1)
    gate_part = jnp.dot(xn_half, w_gate, preferred_element_type=jnp.float32)
    up_part = jnp.dot(xn_half, w_up, preferred_element_type=jnp.float32)
    gate, up = lax.psum((gate_part, up_part), "heads")
    hidden = (jax.nn.silu(gate) * up * route[:, None]).astype(jnp.bfloat16)
    full_term = jnp.dot(hidden, w_down, preferred_element_type=jnp.float32)
    own_start = unit_index * own_rows
    own_h1 = lax.dynamic_slice_in_dim(
        lax.dynamic_slice_in_dim(h1, own_start, own_rows, 0), head_index * half_width, half_width, 1
    )
    own_routed = lax.dynamic_slice_in_dim(is_routed, own_start, own_rows, 0)
    own_slot = jnp.maximum(lax.dynamic_slice_in_dim(slot_of, own_start, own_rows, 0), 0)
    moe_sel = lax.psum(full_term, "units")
    moe_own = jnp.where(own_routed[:, None], moe_sel[own_slot], 0.0)
    return (own_h1.astype(jnp.float32) + moe_own).astype(jnp.bfloat16)


def begin_kernel(o_ref):
    o_ref[...] = jnp.zeros(o_ref.shape, F32)


def attn_kernel(begun_ref, len_ref, table_ref, q_ref, fk_ref, fv_ref, k_ref, v_ref, o_ref):
    pages, page_tokens, kv_width = k_ref.shape
    heads_kv = kv_width // HEAD_WIDTH
    group = q_ref.shape[1] // kv_width
    rows = -(-group // 8) * 8
    scale = HEAD_WIDTH ** (-0.5)
    length = len_ref[0]
    pad = [jnp.zeros((rows - group, HEAD_WIDTH), F32)] if rows > group else []
    table = table_ref[...]
    slots = lax.broadcasted_iota(jnp.int32, table.shape, 1)
    tokens = lax.broadcasted_iota(jnp.int32, (rows, page_tokens), 1)
    live = jnp.concatenate(
        [
            tokens + page_tokens * jnp.sum(jnp.where(table == page, slots, 0), axis=1, keepdims=True) < length
            for page in range(pages)
        ],
        axis=1,
    )
    heads = [slice(g * HEAD_WIDTH, (g + 1) * HEAD_WIDTH) for g in range(heads_kv)]
    q = q_ref[...].astype(F32)
    fk = fk_ref[...].astype(F32)
    q_grid = [
        jnp.concatenate(
            [q[:, (g * group + j) * HEAD_WIDTH : (g * group + j + 1) * HEAD_WIDTH] for j in range(group)] + pad,
            axis=0,
        )
        for g in range(heads_kv)
    ]
    owns = [
        jnp.sum(q_g * fk[:, lanes], axis=1, keepdims=True) * scale for q_g, lanes in zip(q_grid, heads)
    ]
    q_grid = [q_g.astype(BF16) for q_g in q_grid]
    scores = [
        lax.dot_general(
            q_g,
            jnp.concatenate([k_ref[page, :, lanes] for page in range(pages)], axis=0),
            (((1,), (1,)), ((), ())),
            preferred_element_type=F32,
        )
        * scale
        for q_g, lanes in zip(q_grid, heads)
    ]
    weights, own_weights = [], []
    for s, own in zip(scores, owns):
        top = jnp.maximum(jnp.max(jnp.where(live, s, -jnp.inf), axis=1, keepdims=True), own)
        prob = jnp.where(live, jnp.exp(s - top), 0.0)
        own_p = jnp.exp(own - top)
        total = jnp.sum(prob, axis=1, keepdims=True) + own_p
        weights.append((prob / total).astype(BF16))
        own_weights.append((own_p / total).astype(BF16).astype(F32))
    fv = fv_ref[...].astype(F32)
    blended = [
        (
            jnp.dot(
                w,
                jnp.concatenate([v_ref[page, :, lanes] for page in range(pages)], axis=0),
                preferred_element_type=F32,
            )
            + own_w * fv[:, lanes]
        )[:group]
        for w, own_w, lanes in zip(weights, own_weights, heads)
    ]
    attn = jnp.concatenate(blended, axis=0).astype(BF16)
    for r in range(o_ref.shape[0]):
        o_ref[r] = attn


def proj_kernel(attn_ref, w_ref, routes_ref, o_ref, slot_ref):
    attn = attn_ref[...].astype(F32)
    x = jnp.concatenate([attn[:, j, :] for j in range(attn.shape[1])], axis=1).astype(BF16)
    o_ref[...] = jnp.dot(x, w_ref[...], preferred_element_type=F32)
    hit = jnp.logical_or(routes_ref[0:1, :] == 0, routes_ref[1:2, :] == 0)
    ids = lax.broadcasted_iota(jnp.int32, hit.shape, 1)
    first = jnp.min(jnp.where(hit, ids, hit.shape[1]), axis=1, keepdims=True)
    last = jnp.max(jnp.where(hit, ids, -1), axis=1, keepdims=True)
    request = lax.broadcasted_iota(jnp.int32, slot_ref.shape, 0)
    lane = lax.broadcasted_iota(jnp.int32, slot_ref.shape, 1)
    marks = jnp.where(request == jnp.where(lane == 0, first, last), 1, 0)
    named = jnp.where(routes_ref[0:1, :] == 0, routes_ref[1:2, :], routes_ref[0:1, :])
    other = [jnp.sum(jnp.where(ids == r, named, 0), axis=1, keepdims=True) for r in (first, last)]
    marks = jnp.where(lane == 2, other[0], jnp.where(lane == 3, other[1], marks))
    slot_ref[...] = marks


def resid_kernel(resid_ref, mine_ref, other_ref, slot_ref, o_ref):
    h1 = (resid_ref[...].astype(F32) + (mine_ref[...] + other_ref[...])).astype(BF16).astype(F32)
    routed = [
        jnp.sum(jnp.where(slot_ref[:, s : s + 1] > 0, h1, 0.0), axis=0, keepdims=True) for s in range(2)
    ]
    for r in range(o_ref.shape[0]):
        own = h1[r : r + 1]
        o_ref[r] = jnp.concatenate(routed + [own, own], axis=0).astype(BF16)


def gate_up(x, w_refs, o_ref, start, stop, at, width):
    for i, w_ref in enumerate(w_refs):
        lanes = slice(i * width + at, i * width + at + stop - start)
        o_ref[:, lanes] = jnp.dot(x, w_ref[:, start:stop], preferred_element_type=F32)


def scales(h1_ref, gain_ref, router_ref, slot_ref):
    gain = gain_ref[...].astype(F32).reshape(1, -1)
    router = router_ref[...].astype(F32)
    expert = lax.broadcasted_iota(jnp.int32, (router.shape[0], 1), 0)
    h = jnp.concatenate([h1_ref[u].astype(F32)[:2] for u in range(h1_ref.shape[0])], axis=1)
    rstd = lax.rsqrt(jnp.mean(h * h, axis=1, keepdims=True) + 1e-05)
    xn = (h * rstd * gain).astype(BF16).astype(F32)
    lane_ids = lax.broadcasted_iota(jnp.int32, (1, LANES), 1)
    rows = []
    for s in range(2):
        logits = jnp.sum(router * xn[s : s + 1], axis=1, keepdims=True)
        other = slot_ref[0:1, 2 + s : 3 + s]
        diff = jnp.sum(
            jnp.where(expert == other, logits, 0.0) - jnp.where(expert == 0, logits, 0.0),
            axis=0,
            keepdims=True,
        )
        route = 1.0 / (1.0 + jnp.exp(diff))
        rows.append(jnp.where(lane_ids == 0, rstd[s : s + 1], route))
    return jnp.concatenate(rows, axis=0)


def first_kernel(
    h1_ref, gain_ref, wg_ref, wu_ref, router_ref, slot_ref, _, gu_ref, x_ref, ahead_ref
):
    units, _, cols = h1_ref.shape
    part = wg_ref.shape[1] // 2
    ahead = ahead_ref.shape[1] // 2
    per_half = units // 2
    head = lax.axis_index("heads")
    half = per_half * cols
    gain = gain_ref[...].astype(F32).reshape(1, -1)
    gain = jnp.where(head == 0, gain[:, :half], gain[:, half:])
    h1 = jnp.concatenate([h1_ref[head * per_half + i].astype(F32)[:2] for i in range(per_half)], axis=1)
    x = (h1 * gain).astype(BF16)
    x_ref[...] = x
    gate_up(x, (wg_ref, wu_ref), gu_ref, 0, part, 0, part)

    @pl.when(head == 1)
    def _():
        gate_up(x_ref[...], (wg_ref, wu_ref), ahead_ref, part, part + ahead, 0, ahead)
        gu_ref[:, 2 * part :] = scales(h1_ref, gain_ref, router_ref, slot_ref)

    @pl.when(head == 0)
    def _():
        ahead_ref[...] = jnp.zeros(ahead_ref.shape, F32)
        gu_ref[:, 2 * part :] = jnp.zeros((gu_ref.shape[0], LANES), F32)


def second_kernel(
    x_ref, wg_ref, wu_ref, h1_ref, ahead_ref, _, gu_ref, own_ref
):
    part = wg_ref.shape[1] // 2
    ahead = ahead_ref.shape[1] // 2
    first_core = lax.axis_index("heads") == 0

    @pl.when(first_core)
    def _():
        gate_up(x_ref[...], (wg_ref, wu_ref), gu_ref, part, part + ahead, 0, part)

    @pl.when(jnp.logical_not(first_core))
    def _():
        gu_ref[:, :ahead] = ahead_ref[:, :ahead]
        gu_ref[:, part : part + ahead] = ahead_ref[:, ahead:]

    gate_up(x_ref[...], (wg_ref, wu_ref), gu_ref, part + ahead, 2 * part, ahead, part)
    units, _, cols = h1_ref.shape
    per_half = units // 2
    head = lax.axis_index("heads")
    for i in range(per_half):
        own_ref[:, i * cols : (i + 1) * cols] = h1_ref[head * per_half + i].astype(F32)[2:3]


def activate(mine_ref, other_ref, stat, part):
    rstd = stat[:, 0:1]
    route = stat[:, 1:2]
    gate = (mine_ref[:, :part] + other_ref[:, :part]) * rstd
    up = (mine_ref[:, part : 2 * part] + other_ref[:, part : 2 * part]) * (rstd * route)
    return (gate / (1.0 + jnp.exp(-gate)) * up).astype(BF16)


def down_first_kernel(mine_ref, other_ref, wd_ref, o_ref, stat_ref):
    part = wd_ref.shape[0] // 2
    stat = mine_ref[:, 2 * part :] + other_ref[:, 2 * part :]
    stat_ref[...] = stat
    act = activate(mine_ref, other_ref, stat, part)
    o_ref[...] = jnp.dot(act, wd_ref[:part, :], preferred_element_type=F32)


def down_second_kernel(mine_ref, other_ref, stat_ref, wd_ref, before_ref, slot_ref, o_ref, full_ref):
    part = wd_ref.shape[0] // 2
    act = activate(mine_ref, other_ref, stat_ref[...], part)
    full = before_ref[...] + jnp.dot(act, wd_ref[part:, :], preferred_element_type=F32)
    for j in range(o_ref.shape[1]):
        for s in range(2):
            full_ref[s, j : j + 1, :] = full[s : s + 1, j * LANES : (j + 1) * LANES]
    for r in range(o_ref.shape[0]):
        block = jnp.where(slot_ref[r : r + 1, 1:2] > 0, full_ref[1], 0.0)
        o_ref[r] = jnp.where(slot_ref[r : r + 1, 0:1] > 0, full_ref[0], block).astype(BF16)


def sum_kernel(parts_ref, own_ref, o_ref):
    moe = parts_ref[0].astype(F32)
    for u in range(1, parts_ref.shape[0]):
        moe = moe + parts_ref[u].astype(F32)
    for j in range(parts_ref.shape[1]):
        lanes = slice(j * LANES, (j + 1) * LANES)
        o_ref[:, lanes] = (own_ref[:, lanes] + moe[j : j + 1, :]).astype(o_ref.dtype)


SMEM = pl.BlockSpec(memory_space=pltpu.SMEM)
VMEM = pl.BlockSpec(memory_space=pltpu.VMEM)
ANY = pl.BlockSpec(memory_space=pltpu.HBM)


def in_hbm(x):
    return pltpu.with_memory_space_constraint(x, pltpu.HBM)


def in_vmem(x):
    return pltpu.with_memory_space_constraint(x, pltpu.VMEM)


def small_body(
    queries,
    fresh_key,
    fresh_value,
    key_cache_pages,
    value_cache_pages,
    page_table,
    lengths,
    resid,
    w_out,
    norm_gain,
    router,
    routes,
    w_gate,
    w_up,
    w_down,
):
    rows = routes.shape[0]
    half = w_gate.shape[0]
    chunks = half // LANES
    hidden = w_gate.shape[1]
    cols = w_out.shape[1]
    swap = [(0, 1), (1, 0)]
    routes_t = routes.T

    def exchange(x):
        return lax.all_to_all(x, "units", split_axis=0, concat_axis=0, tiled=True)

    def call(kernel, out, specs, name, scratch=(), limit=6, more=()):
        more = [in_hbm(w) for w in more]

        def whole(*refs):
            n = len(specs)
            kernel(*refs[:n], *refs[n + len(more):])

        f = pl.pallas_call(
            whole,
            out_shape=out,
            in_specs=specs + [ANY] * len(more),
            out_specs=jax.tree.map(lambda _: VMEM, out),
            scratch_shapes=scratch,
            compiler_params=pltpu.CompilerParams(vmem_limit_bytes=limit * MIB),
            name=name,
        )
        return lambda *ops: f(*ops, *more)

    begun = call(
        begin_kernel, jax.ShapeDtypeStruct((8, LANES), F32), [], "begin", more=(w_gate,)
    )()
    attn = call(
        attn_kernel,
        jax.ShapeDtypeStruct((rows, chunks, LANES), BF16),
        [VMEM, SMEM] + [VMEM] * 6,
        "attend",
        more=(w_gate, w_up, w_down),
    )(
        begun, lengths, *map(in_vmem, (page_table, queries, fresh_key, fresh_value, key_cache_pages, value_cache_pages)),
    )
    attn_all = exchange(attn)
    proj, slots = call(
        proj_kernel,
        (jax.ShapeDtypeStruct((rows, cols), F32), jax.ShapeDtypeStruct((rows, LANES), jnp.int32)),
        [VMEM] * 3,
        "proj",
    )(attn_all, in_vmem(w_out), routes_t)
    proj_other = lax.ppermute(proj, "heads", swap)
    h1_cols = call(resid_kernel, jax.ShapeDtypeStruct((rows, 4, cols), BF16), [VMEM] * 4, "resid")(
        resid, proj, proj_other, slots
    )
    h1 = exchange(h1_cols)
    weights = (in_vmem(w_gate), in_vmem(w_up))
    w_down_near = in_vmem(w_down)
    gu, x, ahead = call(
        first_kernel,
        (
            jax.ShapeDtypeStruct((2, hidden + LANES), F32),
            jax.ShapeDtypeStruct((2, half), BF16),
            jax.ShapeDtypeStruct((2, 2 * AHEAD_PARTS * (hidden // 16)), F32),
        ),
        [VMEM] * 7,
        "first",
    )(h1, norm_gain, *weights, router.T, slots, w_down_near)
    gu_other = lax.ppermute(gu, "heads", swap)
    gu_late, own_h1 = call(
        second_kernel,
        (jax.ShapeDtypeStruct((2, hidden), F32), jax.ShapeDtypeStruct((1, half), F32)),
        [VMEM] * 6,
        "second",
    )(x, *weights, h1, ahead, w_down_near)
    gu_late_other = lax.ppermute(gu_late, "heads", swap)
    before, stat = call(
        down_first_kernel,
        (jax.ShapeDtypeStruct((2, half), F32), jax.ShapeDtypeStruct((2, LANES), F32)),
        [VMEM] * 3,
        "down_first",
    )(gu, gu_other, w_down_near)
    full = call(
        down_second_kernel,
        jax.ShapeDtypeStruct((rows, chunks, LANES), BF16),
        [VMEM] * 6,
        "down_second",
        scratch=(pltpu.VMEM((2, chunks, LANES), F32),),
    )(gu_late, gu_late_other, stat, w_down_near, before, slots)
    parts = exchange(full)
    return call(sum_kernel, jax.ShapeDtypeStruct((1, half), BF16), [VMEM] * 2, "total")(
        parts, own_h1
    )


def one_tile(*args):
    queries, routes, router = args[0], args[11], args[10]
    rows = routes.shape[0]
    units = lax.axis_size("units")
    return (
        queries.shape[0] == 1
        and rows == 8
        and units == rows
        and rows * routes.shape[1] // router.shape[1] == 2
    )


def dispatch(*args):
    return small_body(*args) if one_tile(*args) else body(*args)


def solution(mesh):
    in_specs = (
        P(("groups", "units"), "heads"),
        P(("groups", "units"), "heads"),
        P(("groups", "units"), "heads"),
        P(("groups", "units"), None, "heads"),
        P(("groups", "units"), None, "heads"),
        P(("groups", "units"), None),
        P(("groups", "units")),
        P("groups", "units"),
        P("heads", "units"),
        P(),
        P(),
        P("groups", None),
        P("heads", "units"),
        P("heads", "units"),
        P("units", "heads"),
    )
    out_specs = P(("groups", "units"), "heads")
    return jax.shard_map(dispatch, mesh=mesh, in_specs=in_specs, out_specs=out_specs, check_vma=False)
```

```python
import functools

import jax
import jax.numpy as jnp
from jax import lax
from jax.experimental import pallas as pl
from jax.experimental.pallas import tpu as pltpu
from jax.sharding import PartitionSpec as P

HEAD_WIDTH = 128
LANES = 128
F32 = jnp.float32
BF16 = jnp.bfloat16
MIB = 2**20
AHEAD_PARTS = 4


def attend(
    queries, fresh_key, fresh_value, key_cache_pages, value_cache_pages, page_table, lengths
):
    token_rows = queries.shape[0]
    kv_width = fresh_key.shape[1]
    heads_kv = kv_width // HEAD_WIDTH
    query_group = queries.shape[1] // kv_width
    score_scale = HEAD_WIDTH ** (-0.5)
    key_rows = key_cache_pages[page_table].reshape(token_rows, -1, heads_kv, HEAD_WIDTH)
    value_rows = value_cache_pages[page_table].reshape(token_rows, -1, heads_kv, HEAD_WIDTH)
    query_grid = queries.reshape(token_rows, heads_kv, query_group, HEAD_WIDTH)
    scores = (
        jnp.einsum("rgjd,rtgd->rgjt", query_grid, key_rows, preferred_element_type=jnp.float32)
        * score_scale
    )
    expert_owned = (
        jnp.einsum(
            "fiam,fim->fia",
            query_grid,
            fresh_key.reshape(token_rows, heads_kv, HEAD_WIDTH),
            preferred_element_type=jnp.float32,
        )
        * score_scale
    )
    span = key_rows.shape[1]
    live = (jnp.arange(span, dtype=jnp.int32)[None, :] < lengths[:, None])[:, None, None, :]
    top = jnp.maximum(jnp.max(jnp.where(live, scores, -jnp.inf), axis=-1), expert_owned)
    prob = jnp.where(live, jnp.exp(scores - top[..., None]), 0.0)
    own_p = jnp.exp(expert_owned - top)
    total = jnp.sum(prob, axis=-1) + own_p
    weights = (prob / total[..., None]).astype(jnp.bfloat16)
    owned_weight = (own_p / total).astype(jnp.bfloat16)
    blended_values = jnp.einsum(
        "rgjt,rtgd->rgjd", weights, value_rows, preferred_element_type=jnp.float32
    )
    blended_values = blended_values + owned_weight.astype(jnp.float32)[
        ..., None
    ] * fresh_value.reshape(token_rows, heads_kv, 1, HEAD_WIDTH).astype(jnp.float32)
    return blended_values.reshape(token_rows, -1).astype(jnp.bfloat16)


def route_weight(logits, routes):
    picks = (
        routes[:, :, None] == jnp.arange(logits.shape[1], dtype=jnp.int32)[None, None, :]
    ).astype(jnp.float32)
    chosen = jnp.sum(picks * logits[:, None, :], axis=-1)
    first = jax.nn.sigmoid(chosen[:, 0] - chosen[:, 1])
    second = jax.nn.sigmoid(chosen[:, 1] - chosen[:, 0])
    return jnp.where(routes[:, 0] == 0, first, jnp.where(routes[:, 1] == 0, second, 0.0))


def body(
    queries,
    fresh_key,
    fresh_value,
    key_cache_pages,
    value_cache_pages,
    page_table,
    lengths,
    resid,
    w_out,
    norm_gain,
    router,
    routes,
    w_gate,
    w_up,
    w_down,
):
    own_rows = queries.shape[0]
    half_width = w_gate.shape[0]
    all_rows = routes.shape[0]
    routed_count = all_rows * routes.shape[1] // router.shape[1]
    unit_index = lax.axis_index("units")
    head_index = lax.axis_index("heads")
    attn = attend(
        queries, fresh_key, fresh_value, key_cache_pages, value_cache_pages, page_table, lengths
    )
    proj_part = jnp.dot(
        lax.all_gather(attn, "units", axis=0, tiled=True), w_out, preferred_element_type=jnp.float32
    )
    proj = lax.psum(proj_part, "heads")
    h1_cols = (resid.astype(jnp.float32) + proj).astype(jnp.bfloat16)
    h1 = lax.all_gather(h1_cols, "units", axis=1, tiled=True)
    is_routed = jnp.any(routes == 0, axis=1)
    slot_of = jnp.cumsum(is_routed.astype(jnp.int32)) - 1
    slot_ids = jnp.arange(routed_count, dtype=jnp.int32)
    row_ids = jnp.arange(all_rows, dtype=jnp.int32)
    match = (slot_of[None, :] == slot_ids[:, None]) & is_routed[None, :]
    picked_rows = jnp.sum(jnp.where(match, row_ids[None, :], 0), axis=1)
    h1_sel = h1[picked_rows]
    hf_sel = h1_sel.astype(jnp.float32)
    rstd = lax.rsqrt(jnp.mean(hf_sel * hf_sel, axis=-1, keepdims=True) + 1e-05)
    xn_sel = (hf_sel * rstd * norm_gain.astype(jnp.float32)).astype(jnp.bfloat16)
    logits = jnp.dot(xn_sel, router, preferred_element_type=jnp.float32)
    route = route_weight(logits, routes[picked_rows])
    xn_half = lax.dynamic_slice_in_dim(xn_sel, head_index * half_width, half_width, 1)
    gate_part = jnp.dot(xn_half, w_gate, preferred_element_type=jnp.float32)
    up_part = jnp.dot(xn_half, w_up, preferred_element_type=jnp.float32)
    gate, up = lax.psum((gate_part, up_part), "heads")
    hidden = (jax.nn.silu(gate) * up * route[:, None]).astype(jnp.bfloat16)
    full_term = jnp.dot(hidden, w_down, preferred_element_type=jnp.float32)
    own_start = unit_index * own_rows
    own_h1 = lax.dynamic_slice_in_dim(
        lax.dynamic_slice_in_dim(h1, own_start, own_rows, 0), head_index * half_width, half_width, 1
    )
    own_routed = lax.dynamic_slice_in_dim(is_routed, own_start, own_rows, 0)
    own_slot = jnp.maximum(lax.dynamic_slice_in_dim(slot_of, own_start, own_rows, 0), 0)
    moe_sel = lax.psum(full_term, "units")
    moe_own = jnp.where(own_routed[:, None], moe_sel[own_slot], 0.0)
    return (own_h1.astype(jnp.float32) + moe_own).astype(jnp.bfloat16)


def begin_kernel(o_ref):
    o_ref[...] = jnp.zeros(o_ref.shape, F32)


def attn_kernel(begun_ref, len_ref, table_ref, q_ref, fk_ref, fv_ref, k_ref, v_ref, o_ref):
    pages, page_tokens, kv_width = k_ref.shape
    heads_kv = kv_width // HEAD_WIDTH
    group = q_ref.shape[1] // kv_width
    rows = -(-group // 8) * 8
    scale = HEAD_WIDTH ** (-0.5)
    length = len_ref[0]
    pad = [jnp.zeros((rows - group, HEAD_WIDTH), F32)] if rows > group else []
    table = table_ref[...]
    slots = lax.broadcasted_iota(jnp.int32, table.shape, 1)
    tokens = lax.broadcasted_iota(jnp.int32, (rows, page_tokens), 1)
    live = jnp.concatenate(
        [
            tokens + page_tokens * jnp.sum(jnp.where(table == page, slots, 0), axis=1, keepdims=True) < length
            for page in range(pages)
        ],
        axis=1,
    )
    heads = [slice(g * HEAD_WIDTH, (g + 1) * HEAD_WIDTH) for g in range(heads_kv)]
    q = q_ref[...].astype(F32)
    fk = fk_ref[...].astype(F32)
    q_grid = [
        jnp.concatenate(
            [q[:, (g * group + j) * HEAD_WIDTH : (g * group + j + 1) * HEAD_WIDTH] for j in range(group)] + pad,
            axis=0,
        )
        for g in range(heads_kv)
    ]
    owns = [
        jnp.sum(q_g * fk[:, lanes], axis=1, keepdims=True) * scale for q_g, lanes in zip(q_grid, heads)
    ]
    q_grid = [q_g.astype(BF16) for q_g in q_grid]
    scores = [
        lax.dot_general(
            q_g,
            jnp.concatenate([k_ref[page, :, lanes] for page in range(pages)], axis=0),
            (((1,), (1,)), ((), ())),
            preferred_element_type=F32,
        )
        * scale
        for q_g, lanes in zip(q_grid, heads)
    ]
    weights, own_weights = [], []
    for s, own in zip(scores, owns):
        top = jnp.maximum(jnp.max(jnp.where(live, s, -jnp.inf), axis=1, keepdims=True), own)
        prob = jnp.where(live, jnp.exp(s - top), 0.0)
        own_p = jnp.exp(own - top)
        total = jnp.sum(prob, axis=1, keepdims=True) + own_p
        weights.append((prob / total).astype(BF16))
        own_weights.append((own_p / total).astype(BF16).astype(F32))
    fv = fv_ref[...].astype(F32)
    blended = [
        (
            jnp.dot(
                w,
                jnp.concatenate([v_ref[page, :, lanes] for page in range(pages)], axis=0),
                preferred_element_type=F32,
            )
            + own_w * fv[:, lanes]
        )[:group]
        for w, own_w, lanes in zip(weights, own_weights, heads)
    ]
    attn = jnp.concatenate(blended, axis=0).astype(BF16)
    for r in range(o_ref.shape[0]):
        o_ref[r] = attn


def proj_kernel(attn_ref, w_ref, routes_ref, o_ref, slot_ref):
    attn = attn_ref[...].astype(F32)
    x = jnp.concatenate([attn[:, j, :] for j in range(attn.shape[1])], axis=1).astype(BF16)
    o_ref[...] = jnp.dot(x, w_ref[...], preferred_element_type=F32)
    hit = jnp.logical_or(routes_ref[0:1, :] == 0, routes_ref[1:2, :] == 0)
    ids = lax.broadcasted_iota(jnp.int32, hit.shape, 1)
    first = jnp.min(jnp.where(hit, ids, hit.shape[1]), axis=1, keepdims=True)
    last = jnp.max(jnp.where(hit, ids, -1), axis=1, keepdims=True)
    request = lax.broadcasted_iota(jnp.int32, slot_ref.shape, 0)
    lane = lax.broadcasted_iota(jnp.int32, slot_ref.shape, 1)
    marks = jnp.where(request == jnp.where(lane == 0, first, last), 1, 0)
    named = jnp.where(routes_ref[0:1, :] == 0, routes_ref[1:2, :], routes_ref[0:1, :])
    other = [jnp.sum(jnp.where(ids == r, named, 0), axis=1, keepdims=True) for r in (first, last)]
    marks = jnp.where(lane == 2, other[0], jnp.where(lane == 3, other[1], marks))
    slot_ref[...] = marks


def resid_kernel(resid_ref, mine_ref, other_ref, slot_ref, o_ref):
    h1 = (resid_ref[...].astype(F32) + (mine_ref[...] + other_ref[...])).astype(BF16).astype(F32)
    routed = [
        jnp.sum(jnp.where(slot_ref[:, s : s + 1] > 0, h1, 0.0), axis=0, keepdims=True) for s in range(2)
    ]
    for r in range(o_ref.shape[0]):
        own = h1[r : r + 1]
        o_ref[r] = jnp.concatenate(routed + [own, own], axis=0).astype(BF16)


def gate_up(x, w_refs, o_ref, start, stop, at, width):
    for i, w_ref in enumerate(w_refs):
        lanes = slice(i * width + at, i * width + at + stop - start)
        o_ref[:, lanes] = jnp.dot(x, w_ref[:, start:stop], preferred_element_type=F32)


def scales(h1_ref, gain_ref, router_ref, slot_ref):
    gain = gain_ref[...].astype(F32).reshape(1, -1)
    router = router_ref[...].astype(F32)
    expert = lax.broadcasted_iota(jnp.int32, (router.shape[0], 1), 0)
    h = jnp.concatenate([h1_ref[u].astype(F32)[:2] for u in range(h1_ref.shape[0])], axis=1)
    rstd = lax.rsqrt(jnp.mean(h * h, axis=1, keepdims=True) + 1e-05)
    xn = (h * rstd * gain).astype(BF16).astype(F32)
    lane_ids = lax.broadcasted_iota(jnp.int32, (1, LANES), 1)
    rows = []
    for s in range(2):
        logits = jnp.sum(router * xn[s : s + 1], axis=1, keepdims=True)
        other = slot_ref[0:1, 2 + s : 3 + s]
        diff = jnp.sum(
            jnp.where(expert == other, logits, 0.0) - jnp.where(expert == 0, logits, 0.0),
            axis=0,
            keepdims=True,
        )
        route = 1.0 / (1.0 + jnp.exp(diff))
        rows.append(jnp.where(lane_ids == 0, rstd[s : s + 1], route))
    return jnp.concatenate(rows, axis=0)


def first_kernel(
    h1_ref, gain_ref, wg_ref, wu_ref, router_ref, slot_ref, _, gu_ref, x_ref, ahead_ref
):
    units, _, cols = h1_ref.shape
    part = wg_ref.shape[1] // 2
    ahead = ahead_ref.shape[1] // 2
    per_half = units // 2
    head = lax.axis_index("heads")
    half = per_half * cols
    gain = gain_ref[...].astype(F32).reshape(1, -1)
    gain = jnp.where(head == 0, gain[:, :half], gain[:, half:])
    h1 = jnp.concatenate([h1_ref[head * per_half + i].astype(F32)[:2] for i in range(per_half)], axis=1)
    x = (h1 * gain).astype(BF16)
    x_ref[...] = x
    gate_up(x, (wg_ref, wu_ref), gu_ref, 0, part, 0, part)

    @pl.when(head == 1)
    def _():
        gate_up(x_ref[...], (wg_ref, wu_ref), ahead_ref, part, part + ahead, 0, ahead)
        gu_ref[:, 2 * part :] = scales(h1_ref, gain_ref, router_ref, slot_ref)

    @pl.when(head == 0)
    def _():
        ahead_ref[...] = jnp.zeros(ahead_ref.shape, F32)
        gu_ref[:, 2 * part :] = jnp.zeros((gu_ref.shape[0], LANES), F32)


def second_kernel(
    x_ref, wg_ref, wu_ref, h1_ref, ahead_ref, _, gu_ref, own_ref
):
    part = wg_ref.shape[1] // 2
    ahead = ahead_ref.shape[1] // 2
    first_core = lax.axis_index("heads") == 0

    @pl.when(first_core)
    def _():
        gate_up(x_ref[...], (wg_ref, wu_ref), gu_ref, part, part + ahead, 0, part)

    @pl.when(jnp.logical_not(first_core))
    def _():
        gu_ref[:, :ahead] = ahead_ref[:, :ahead]
        gu_ref[:, part : part + ahead] = ahead_ref[:, ahead:]

    gate_up(x_ref[...], (wg_ref, wu_ref), gu_ref, part + ahead, 2 * part, ahead, part)
    units, _, cols = h1_ref.shape
    per_half = units // 2
    head = lax.axis_index("heads")
    for i in range(per_half):
        own_ref[:, i * cols : (i + 1) * cols] = h1_ref[head * per_half + i].astype(F32)[2:3]


def activate(mine_ref, other_ref, stat, part):
    rstd = stat[:, 0:1]
    route = stat[:, 1:2]
    gate = (mine_ref[:, :part] + other_ref[:, :part]) * rstd
    up = (mine_ref[:, part : 2 * part] + other_ref[:, part : 2 * part]) * (rstd * route)
    return (gate / (1.0 + jnp.exp(-gate)) * up).astype(BF16)


def down_first_kernel(mine_ref, other_ref, wd_ref, o_ref, stat_ref):
    part = wd_ref.shape[0] // 2
    stat = mine_ref[:, 2 * part :] + other_ref[:, 2 * part :]
    stat_ref[...] = stat
    act = activate(mine_ref, other_ref, stat, part)
    o_ref[...] = jnp.dot(act, wd_ref[:part, :], preferred_element_type=F32)


def down_second_kernel(mine_ref, other_ref, stat_ref, wd_ref, before_ref, slot_ref, o_ref, full_ref):
    part = wd_ref.shape[0] // 2
    act = activate(mine_ref, other_ref, stat_ref[...], part)
    full = before_ref[...] + jnp.dot(act, wd_ref[part:, :], preferred_element_type=F32)
    for j in range(o_ref.shape[1]):
        for s in range(2):
            full_ref[s, j : j + 1, :] = full[s : s + 1, j * LANES : (j + 1) * LANES]
    for r in range(o_ref.shape[0]):
        block = jnp.where(slot_ref[r : r + 1, 1:2] > 0, full_ref[1], 0.0)
        o_ref[r] = jnp.where(slot_ref[r : r + 1, 0:1] > 0, full_ref[0], block).astype(BF16)


def sum_kernel(parts_ref, own_ref, o_ref):
    moe = parts_ref[0].astype(F32)
    for u in range(1, parts_ref.shape[0]):
        moe = moe + parts_ref[u].astype(F32)
    flat = jnp.concatenate([moe[j : j + 1, :] for j in range(parts_ref.shape[1])], axis=1)
    o_ref[...] = (own_ref[...] + flat).astype(o_ref.dtype)


SMEM = pl.BlockSpec(memory_space=pltpu.SMEM)
VMEM = pl.BlockSpec(memory_space=pltpu.VMEM)
ANY = pl.BlockSpec(memory_space=pltpu.HBM)


def in_hbm(x):
    return pltpu.with_memory_space_constraint(x, pltpu.HBM)


def in_vmem(x):
    return pltpu.with_memory_space_constraint(x, pltpu.VMEM)


def small_body(
    queries,
    fresh_key,
    fresh_value,
    key_cache_pages,
    value_cache_pages,
    page_table,
    lengths,
    resid,
    w_out,
    norm_gain,
    router,
    routes,
    w_gate,
    w_up,
    w_down,
):
    rows = routes.shape[0]
    half = w_gate.shape[0]
    chunks = half // LANES
    hidden = w_gate.shape[1]
    cols = w_out.shape[1]
    swap = [(0, 1), (1, 0)]
    routes_t = routes.T

    def exchange(x):
        return lax.all_to_all(x, "units", split_axis=0, concat_axis=0, tiled=True)

    def call(kernel, out, specs, name, scratch=(), limit=6, more=()):
        more = [in_hbm(w) for w in more]

        def whole(*refs):
            n = len(specs)
            kernel(*refs[:n], *refs[n + len(more):])

        f = pl.pallas_call(
            whole,
            out_shape=out,
            in_specs=specs + [ANY] * len(more),
            out_specs=jax.tree.map(lambda _: VMEM, out),
            scratch_shapes=scratch,
            compiler_params=pltpu.CompilerParams(vmem_limit_bytes=limit * MIB),
            name=name,
        )
        return lambda *ops: f(*ops, *more)

    begun = call(
        begin_kernel, jax.ShapeDtypeStruct((8, LANES), F32), [], "begin", more=(w_gate,)
    )()
    attn = call(
        attn_kernel,
        jax.ShapeDtypeStruct((rows, chunks, LANES), BF16),
        [VMEM, SMEM] + [VMEM] * 6,
        "attend",
        more=(w_gate, w_up, w_down),
    )(
        begun, lengths, *map(in_vmem, (page_table, queries, fresh_key, fresh_value, key_cache_pages, value_cache_pages)),
    )
    attn_all = exchange(attn)
    proj, slots = call(
        proj_kernel,
        (jax.ShapeDtypeStruct((rows, cols), F32), jax.ShapeDtypeStruct((rows, LANES), jnp.int32)),
        [VMEM] * 3,
        "proj",
    )(attn_all, in_vmem(w_out), routes_t)
    proj_other = lax.ppermute(proj, "heads", swap)
    h1_cols = call(resid_kernel, jax.ShapeDtypeStruct((rows, 4, cols), BF16), [VMEM] * 4, "resid")(
        resid, proj, proj_other, slots
    )
    h1 = exchange(h1_cols)
    weights = (in_vmem(w_gate), in_vmem(w_up))
    w_down_near = in_vmem(w_down)
    gu, x, ahead = call(
        first_kernel,
        (
            jax.ShapeDtypeStruct((2, hidden + LANES), F32),
            jax.ShapeDtypeStruct((2, half), BF16),
            jax.ShapeDtypeStruct((2, 2 * AHEAD_PARTS * (hidden // 16)), F32),
        ),
        [VMEM] * 7,
        "first",
    )(h1, norm_gain, *weights, router.T, slots, w_down_near)
    gu_other = lax.ppermute(gu, "heads", swap)
    gu_late, own_h1 = call(
        second_kernel,
        (jax.ShapeDtypeStruct((2, hidden), F32), jax.ShapeDtypeStruct((1, half), F32)),
        [VMEM] * 6,
        "second",
    )(x, *weights, h1, ahead, w_down_near)
    gu_late_other = lax.ppermute(gu_late, "heads", swap)
    before, stat = call(
        down_first_kernel,
        (jax.ShapeDtypeStruct((2, half), F32), jax.ShapeDtypeStruct((2, LANES), F32)),
        [VMEM] * 3,
        "down_first",
    )(gu, gu_other, w_down_near)
    full = call(
        down_second_kernel,
        jax.ShapeDtypeStruct((rows, chunks, LANES), BF16),
        [VMEM] * 6,
        "down_second",
        scratch=(pltpu.VMEM((2, chunks, LANES), F32),),
    )(gu_late, gu_late_other, stat, w_down_near, before, slots)
    parts = exchange(full)
    return call(sum_kernel, jax.ShapeDtypeStruct((1, half), BF16), [VMEM] * 2, "total")(
        parts, own_h1
    )


def one_tile(*args):
    queries, routes, router = args[0], args[11], args[10]
    rows = routes.shape[0]
    units = lax.axis_size("units")
    return (
        queries.shape[0] == 1
        and rows == 8
        and units == rows
        and rows * routes.shape[1] // router.shape[1] == 2
    )


def dispatch(*args):
    return small_body(*args) if one_tile(*args) else body(*args)


def solution(mesh):
    in_specs = (
        P(("groups", "units"), "heads"),
        P(("groups", "units"), "heads"),
        P(("groups", "units"), "heads"),
        P(("groups", "units"), None, "heads"),
        P(("groups", "units"), None, "heads"),
        P(("groups", "units"), None),
        P(("groups", "units")),
        P("groups", "units"),
        P("heads", "units"),
        P(),
        P(),
        P("groups", None),
        P("heads", "units"),
        P("heads", "units"),
        P("units", "heads"),
    )
    out_specs = P(("groups", "units"), "heads")
    return jax.shard_map(dispatch, mesh=mesh, in_specs=in_specs, out_specs=out_specs, check_vma=False)
```
